32 devices in a mesh: depth: 8 (over z, x), strip: 4 (over y, core).
Axes of the slice: x: 2, y: 2, z: 4, core: 2. Of those that a mesh axis runs over, the one named last changes fastest.
Arguments:
- density: bfloat16 [32, 64, 1024], P('depth', 'strip'), may hold values from -6 to 6
- tf_bins: int32 [32, 64, 1024], P('depth', 'strip'), may hold values from 0 to 15
- tf_table: float32 [4, 16], replicated, may hold values from 0.2 to 2
- brick_order: int32 [4, 8], P('strip'), may hold values from 0 to 7, each once within a row
Outputs:
- image: float32 [4, 65536], P(None, ('strip', 'depth'))
The draws below stay inside these ranges and needn't reach their ends.
Inputs may be any that keep to these rules, and one draw needn't show every extreme that they name: `tf_bins`: each voxel's bin indexes a column of tf_table. `brick_order`: each row lists every brick once.
All inputs are finite; a program needn't handle non-finite values.
Results may differ from the reference program's by a relative error of at most 0.0017.
Values may be sent and summed in bfloat16 or wider, within the bound.
No kernel may reach another device: no remote copies, remote signals or barrier semaphores. Data moves between devices by JAX's collectives and lax.ppermute only.
A program may use at most 64 MiB of HBM per device.

```python
import math
import jax
import jax.numpy as jnp
from jax import lax

PLANES = 4
ROWS_DEV = 16
NX = 1024
CLASSES = 16
BRICKS = 8
STRIPS = 4
NZ = 32
IMG_ROWS = 64


def touch_ends(entries, rng, low, high):
    extent = entries.shape
    spot = [jax.random.randint(jax.random.fold_in(rng, axis), (), 0, extent[axis]) for axis in range(len(extent))]
    entries = entries.at[tuple(spot)].set(low)
    longest = extent.index(max(extent))
    spot[longest] = (spot[longest] + 1) % extent[longest]
    return entries.at[tuple(spot)].set(high)


def levels(rng, dims, pieces, low, top_value):
    gain, own = 1.0, jax.random.fold_in(rng, 6)
    for dim, blocks in pieces:
        heights = jnp.exp(jax.random.uniform(jax.random.fold_in(own, dim), (blocks,), jnp.float32, low / len(pieces), top_value / len(pieces)))
        gain = gain * jnp.repeat(heights, dims[dim] // blocks).reshape([-1 if axis == dim else 1 for axis in range(len(dims))])
    return gain


def scatter_about(rng, extent, spread, limit, split=(), kind=jnp.bfloat16):
    entries = spread * jax.random.normal(rng, extent, jnp.float32)
    if split:
        entries = entries * levels(rng, extent, split, -0.22, 0.18)
    return jnp.clip(entries, -limit, limit).astype(kind)


def setup_inputs(seed: int = 0) -> dict:
    splits = jax.random.split(jax.random.key(seed), 5)
    density = scatter_about(splits[0], (NZ, IMG_ROWS, NX), 1.0, 6.0, ((0, 8), (1, 4)))
    tf_bins = touch_ends(jax.random.randint(splits[1], (NZ, IMG_ROWS, NX), 0, CLASSES), jax.random.fold_in(splits[1], 1), 0, CLASSES - 1).astype(jnp.int32)
    tf_table = jnp.clip(jnp.exp(jax.random.uniform(splits[2], (4, CLASSES), jnp.float32, math.log(0.2), math.log(2.0))), 0.2, 2.0)
    brick_order = jax.vmap(lambda own: jax.random.permutation(own, BRICKS))(jax.random.split(splits[3], STRIPS)).reshape((STRIPS, BRICKS)).astype(jnp.int32)
    return {"density": density, "tf_bins": tf_bins, "tf_table": tf_table, "brick_order": brick_order}


LIGHT_X = 0.36
LIGHT_Y = 0.48
LIGHT_Z = 0.8
SHADE_GAIN = 1.5

def shear_plane(values, plane_index):
    across = values.shape[-1]
    offset = (3 * plane_index // 8).astype(jnp.int32)
    fraction = (3 * plane_index % 8).astype(jnp.float32) / 8.0
    columns = jnp.arange(across, dtype=jnp.int32)
    first = jnp.where(columns < across - offset, jnp.roll(values, -offset, axis=2), 0.0)
    second = jnp.where(columns < across - offset - 1, jnp.roll(first, -1, axis=2), 0.0)
    return (1.0 - fraction) * first + fraction * second

def plane_terms(window, tf_plane, tf_table, plane_index, total_planes):
    beneath = window[0]
    middle = window[1]
    overhead = window[2]
    centre = middle[1:-1]
    sideways = jnp.pad(centre, ((0, 0), (1, 1)))
    slope_across = 0.5 * (sideways[:, 2:] - sideways[:, :-2])
    slope_down = 0.5 * (middle[2:] - middle[:-2])
    slope_deep = 0.5 * (overhead[1:-1] - beneath[1:-1])
    lengths = jnp.sqrt(1.0 + slope_across * slope_across + slope_down * slope_down + slope_deep * slope_deep)
    shading = (LIGHT_X * slope_across + LIGHT_Y * slope_down + LIGHT_Z * slope_deep) / lengths
    classes = jnp.arange(tf_table.shape[1], dtype=jnp.int32)
    onehot = (tf_plane[None, :, :] == classes[:, None, None]).astype(jnp.float32)
    looked = jnp.einsum('cm,myx->cyx', tf_table, onehot, precision=lax.Precision.HIGHEST)
    extinction = looked[0] * (1.0 + centre * centre) / total_planes
    opacity = 1.0 - jnp.exp(-extinction)
    emitted = looked[1:] * (opacity * jnp.exp(SHADE_GAIN * shading))[None]
    return shear_plane(jnp.concatenate([extinction[None], emitted], axis=0), plane_index)

def brick_terms(block, tf_brick, tf_table, first_plane, total_planes):
    height = block.shape[1] - 2
    across = block.shape[2]

    def advance(running, plane_at):
        colour, depth_sum = running
        window = lax.dynamic_slice_in_dim(block, plane_at, 3, 0)
        tf_plane = lax.dynamic_index_in_dim(tf_brick, plane_at, 0, keepdims=False)
        sheared = plane_terms(window, tf_plane, tf_table, first_plane + plane_at, total_planes)
        colour = colour + jnp.exp(-depth_sum)[None] * sheared[1:]
        depth_sum = depth_sum + sheared[0]
        return ((colour, depth_sum), None)
    start = (jnp.zeros((3, height, across), jnp.float32), jnp.zeros((height, across), jnp.float32))
    finished, ignored = lax.scan(advance, start, jnp.arange(tf_brick.shape[0], dtype=jnp.int32))
    return finished

def order_mask(sequence):
    bricks = sequence.shape[0]
    slots = jnp.arange(bricks, dtype=jnp.int32)
    onehot = (sequence[:, None] == slots[None, :]).astype(jnp.int32)
    position = lax.optimization_barrier(jnp.sum(onehot * slots[:, None], axis=0))
    return (position[None, :] < position[:, None]).astype(jnp.float32)

def reference(density, tf_bins, tf_table, brick_order):
    padded = jnp.pad(density, ((1, 1), (1, 1), (0, 0)))

    def one_brick(brick):
        first_plane = (brick * PLANES).astype(jnp.int32)
        block = lax.dynamic_slice_in_dim(padded, first_plane, PLANES + 2, 0).astype(jnp.float32)
        tf_brick = lax.dynamic_slice_in_dim(tf_bins, first_plane, PLANES, 0)
        colour, depth_sum = brick_terms(block, tf_brick, tf_table, first_plane, NZ)
        return jnp.concatenate([colour, depth_sum[None]], axis=0)
    layers = lax.map(one_brick, jnp.arange(BRICKS, dtype=jnp.int32))

    def one_strip(strip):
        rows_block = lax.dynamic_slice_in_dim(layers, (strip * ROWS_DEV).astype(jnp.int32), ROWS_DEV, 2)
        before = order_mask(lax.dynamic_index_in_dim(brick_order, strip, 0, keepdims=False))
        depths = rows_block[:, 3]
        prefix = jnp.einsum('ab,byx->ayx', before, depths, precision=lax.Precision.HIGHEST)
        weight = jnp.exp(-prefix)
        shown = lax.optimization_barrier(jnp.sum(weight[:, None] * rows_block[:, :3], axis=0))
        remaining = jnp.exp(-lax.optimization_barrier(jnp.sum(depths, axis=0)))
        return jnp.concatenate([shown, remaining[None]], axis=0)
    strips = lax.map(one_strip, jnp.arange(STRIPS, dtype=jnp.int32))
    return jnp.transpose(strips, (1, 0, 2, 3)).reshape(4, IMG_ROWS * NX)
```

```python
import functools

import jax
import jax.numpy as jnp
from jax import lax
from jax.experimental import pallas as pl
from jax.experimental.pallas import tpu as pltpu
from jax.sharding import PartitionSpec as P

LIGHT = (0.36, 0.48, 0.8)
SHADE_GAIN = 1.5
LOG2E = 1.4426950408889634
LANES = 128

MAX_DENSITY = 6.0
MAX_LOOKED = 2.0

COLOUR_STEPS = 2048.0
COLOUR_LOW = -28.0
CODE_MAX = 65535.0


def depth_scale(planes, total_planes):
    return MAX_LOOKED * (1.0 + MAX_DENSITY * MAX_DENSITY) * LOG2E * planes / total_planes


def pairs(count, start):
    swaps = []
    for i in range(start, count - 1, 2):
        swaps += [(i, i + 1), (i + 1, i)]
    return swaps


def exchange(cells, axis, dim):
    count = lax.axis_size(axis)
    odd = lax.axis_index(axis) % 2 == 1
    size = cells.shape[dim]
    head = lax.slice_in_dim(cells, 0, 1, axis=dim)
    tail = lax.slice_in_dim(cells, size - 1, size, axis=dim)
    near = lax.ppermute(jnp.where(odd, head, tail), axis, pairs(count, 0))
    far = lax.ppermute(jnp.where(odd, tail, head), axis, pairs(count, 1))
    return near, far


def tiles_of(value):
    return [value[:, t : t + LANES] for t in range(0, value.shape[1], LANES)]


def lane_next(tiles, lane):
    rolled = [pltpu.roll(v, LANES - 1, 1) for v in tiles] + [0.0]
    return [jnp.where(lane < LANES - 1, rolled[t], rolled[t + 1]) for t in range(len(tiles))]


def lane_previous(tiles, lane):
    rolled = [0.0] + [pltpu.roll(v, 1, 1) for v in tiles]
    return [jnp.where(lane > 0, rolled[t + 1], rolled[t]) for t in range(len(tiles))]


def lane_shift(tiles, lane, shift):
    amount = (LANES - shift) % LANES
    rolled = [pltpu.roll(v, amount, 1) for v in tiles] + [0.0]
    return [jnp.where(lane < LANES - shift, rolled[t], rolled[t + 1]) for t in range(len(tiles))]


def brick_kernel(
    bricks, density_ref, bins_ref, table_ref, plane_near, plane_far, row_near, row_far, out_ref
):
    planes, height, across = density_ref.shape
    total_planes = planes * bricks
    brick = lax.axis_index("depth")
    odd_brick = brick % 2 == 1
    odd_strip = lax.axis_index("strip") % 2 == 1
    count = across // LANES
    lane = lax.broadcasted_iota(jnp.int32, (height, LANES), 1)
    row = lax.broadcasted_iota(jnp.int32, (height, LANES), 0)
    f32 = jnp.float32

    near, far = plane_near[0].astype(f32), plane_far[0].astype(f32)
    beneath = tiles_of(jnp.where(odd_brick, near, far))
    overhead = tiles_of(jnp.where(odd_brick, far, near))
    near, far = row_near[:, 0, :].astype(f32), row_far[:, 0, :].astype(f32)
    above = jnp.where(odd_strip, near, far)
    below = jnp.where(odd_strip, far, near)
    stack = [beneath]
    stack += [tiles_of(density_ref[p].astype(f32)) for p in range(planes)]
    stack += [overhead]
    table = [
        jnp.broadcast_to(table_ref[c : c + 1, :], (height, LANES)) for c in range(4)
    ]
    table[0] = table[0] * (LOG2E / total_planes)

    depth = [jnp.zeros((height, LANES), f32)] * count
    colour = [[jnp.zeros((height, LANES), f32)] * count for _ in range(3)]
    for p in range(planes):
        plane_index = brick * planes + p
        shift = (3 * plane_index) // 8
        fraction = ((3 * plane_index) % 8).astype(f32) / 8.0
        centre = stack[p + 1]
        ahead, behind = lane_next(centre, lane), lane_previous(centre, lane)
        fields = [[], [], [], []]
        for t in range(count):
            cols = slice(t * LANES, (t + 1) * LANES)
            v = centre[t]
            up = jnp.where(row == 0, above[p : p + 1, cols], pltpu.roll(v, 1, 0))
            down = jnp.where(
                row == height - 1, below[p : p + 1, cols], pltpu.roll(v, height - 1, 0)
            )
            dx = ahead[t] - behind[t]
            dy = down - up
            dz = stack[p + 2][t] - stack[p][t]
            gain = SHADE_GAIN * LOG2E
            lit = (LIGHT[0] * gain) * dx + (LIGHT[1] * gain) * dy + (LIGHT[2] * gain) * dz
            shade = jnp.exp2(lit * lax.rsqrt(4.0 + dx * dx + dy * dy + dz * dz))
            bins = bins_ref[p, :, cols]
            looked = [
                jnp.take_along_axis(entry, bins, axis=1, mode="promise_in_bounds")
                for entry in table
            ]
            extinction = looked[0] * (1.0 + v * v)
            strength = (1.0 - jnp.exp2(-extinction)) * shade
            fields[0].append(extinction)
            for c in range(3):
                fields[c + 1].append(looked[c + 1] * strength)
        sheared = []
        for field in fields:
            first = lane_shift(field, lane, shift)
            second = lane_next(first, lane)
            sheared.append([a + fraction * (b - a) for a, b in zip(first, second)])
        for t in range(count):
            through = jnp.exp2(-depth[t])
            for c in range(3):
                colour[c][t] = colour[c][t] + through * sheared[c + 1][t]
            depth[t] = depth[t] + sheared[0][t]

    depth_factor = CODE_MAX / depth_scale(planes, total_planes)
    words = [[], []]
    for t in range(count):
        codes = [jnp.minimum(depth[t] * depth_factor, CODE_MAX)]
        for c in range(3):
            code = jnp.log2(colour[c][t]) * COLOUR_STEPS - COLOUR_LOW * COLOUR_STEPS
            codes.append(jnp.minimum(jnp.maximum(code, 0.0), CODE_MAX))
        codes = [(code + 0.5).astype(jnp.int32) for code in codes]
        words[0].append(codes[0] | (codes[1] << 16))
        words[1].append(codes[2] | (codes[3] << 16))
    owned = height * across // bricks
    tall, wide = max(owned // across, 1), min(owned, across)
    for owner in range(bricks):
        top, left = owner * owned // across, owner * owned % across
        for w in range(2):
            for t in range(wide // LANES):
                out_ref[owner, w, t * tall : (t + 1) * tall, :] = words[w][left // LANES + t][
                    top : top + tall, :
                ]


def merge_kernel(planes, tall, order_ref, words_ref, out_ref):
    bricks, _, rows, _ = words_ref.shape
    f32 = jnp.float32
    depth_unit = depth_scale(planes, planes * bricks) / CODE_MAX
    passed = jnp.zeros((rows, LANES), f32)
    colour = [jnp.zeros((rows, LANES), f32)] * 3
    for k in range(bricks):
        brick = order_ref[0, k]
        words = [words_ref[brick, 0], words_ref[brick, 1]]
        codes = []
        for word in words:
            codes += [word & 0xFFFF, lax.shift_right_logical(word, 16)]
        base = COLOUR_LOW - passed
        for c in range(3):
            code = codes[c + 1]
            term = jnp.exp2(code.astype(f32) * (1.0 / COLOUR_STEPS) + base)
            colour[c] = colour[c] + jnp.where(code > 0, term, 0.0)
        passed = passed + codes[0].astype(f32) * depth_unit
    image = colour + [jnp.exp2(-passed)]
    wide = rows // tall
    for c in range(4):
        for r in range(tall):
            for t in range(wide):
                at = (r * wide + t) * LANES
                out_ref[c : c + 1, at : at + LANES] = image[c][t * tall + r : t * tall + r + 1, :]


def per_device(density, tf_bins, tf_table, brick_order):
    planes, height, across = density.shape
    bricks = lax.axis_size("depth")
    plane_near, plane_far = exchange(density, "depth", 0)
    row_near, row_far = exchange(density, "strip", 1)
    owned = height * across // bricks
    table = jnp.pad(tf_table, ((0, 0), (0, LANES - tf_table.shape[1])))
    vmem = pl.BlockSpec(memory_space=pltpu.VMEM)
    words = pl.pallas_call(
        functools.partial(brick_kernel, bricks),
        out_shape=jax.ShapeDtypeStruct((bricks, 2, owned // LANES, LANES), jnp.int32),
        in_specs=[vmem] * 7,
        out_specs=vmem,
    )(density, tf_bins, table, plane_near, plane_far, row_near, row_far)
    words = lax.all_to_all(words, "depth", 0, 0, tiled=True)
    return pl.pallas_call(
        functools.partial(merge_kernel, planes, max(owned // across, 1)),
        out_shape=jax.ShapeDtypeStruct((4, owned), jnp.float32),
        in_specs=[pl.BlockSpec(memory_space=pltpu.SMEM), vmem],
        out_specs=vmem,
    )(brick_order, words)


def solution(mesh):
    in_specs = (P("depth", "strip", None), P("depth", "strip", None), P(), P("strip", None))
    out_specs = P(None, ("strip", "depth"))
    return jax.shard_map(
        per_device, mesh=mesh, in_specs=in_specs, out_specs=out_specs, check_vma=False
    )
```

```python
import functools

import jax
import jax.numpy as jnp
from jax import lax
from jax.experimental import pallas as pl
from jax.experimental.pallas import tpu as pltpu
from jax.sharding import PartitionSpec as P

LIGHT = (0.36, 0.48, 0.8)
SHADE_GAIN = 1.5
LOG2E = 1.4426950408889634
LANES = 128
VMEM_BYTES = 8 * 1024 * 1024

MAX_DENSITY = 6.0
MAX_LOOKED = 2.0

COLOUR_STEPS = 2048.0
COLOUR_LOW = -28.0
CODE_MAX = 65535.0


def depth_scale(planes, total_planes):
    return MAX_LOOKED * (1.0 + MAX_DENSITY * MAX_DENSITY) * LOG2E * planes / total_planes


def pairs(count, start):
    swaps = []
    for i in range(start, count - 1, 2):
        swaps += [(i, i + 1), (i + 1, i)]
    return swaps


def exchange(cells, axis, dim):
    count = lax.axis_size(axis)
    odd = lax.axis_index(axis) % 2 == 1
    size = cells.shape[dim]
    head = lax.slice_in_dim(cells, 0, 1, axis=dim)
    tail = lax.slice_in_dim(cells, size - 1, size, axis=dim)
    near = lax.ppermute(jnp.where(odd, head, tail), axis, pairs(count, 0))
    far = lax.ppermute(jnp.where(odd, tail, head), axis, pairs(count, 1))
    return near, far


def tiles_of(value):
    return [value[:, t : t + LANES] for t in range(0, value.shape[1], LANES)]


def lane_next(tiles, lane):
    rolled = [pltpu.roll(v, LANES - 1, 1) for v in tiles] + [0.0]
    return [jnp.where(lane < LANES - 1, rolled[t], rolled[t + 1]) for t in range(len(tiles))]


def lane_previous(tiles, lane):
    rolled = [0.0] + [pltpu.roll(v, 1, 1) for v in tiles]
    return [jnp.where(lane > 0, rolled[t + 1], rolled[t]) for t in range(len(tiles))]


def lane_shift(tiles, lane, shift):
    amount = (LANES - shift) % LANES
    rolled = [pltpu.roll(v, amount, 1) for v in tiles] + [0.0]
    return [jnp.where(lane < LANES - shift, rolled[t], rolled[t + 1]) for t in range(len(tiles))]


def brick_kernel(
    bricks, density_ref, bins_ref, table_ref, plane_near, plane_far, row_near, row_far, out_ref
):
    planes, height, across = density_ref.shape
    total_planes = planes * bricks
    brick = lax.axis_index("depth")
    odd_brick = brick % 2 == 1
    odd_strip = lax.axis_index("strip") % 2 == 1
    count = across // LANES
    lane = lax.broadcasted_iota(jnp.int32, (height, LANES), 1)
    row = lax.broadcasted_iota(jnp.int32, (height, LANES), 0)
    f32 = jnp.float32

    near, far = plane_near[0].astype(f32), plane_far[0].astype(f32)
    beneath = tiles_of(jnp.where(odd_brick, near, far))
    overhead = tiles_of(jnp.where(odd_brick, far, near))
    near, far = row_near[:, 0, :].astype(f32), row_far[:, 0, :].astype(f32)
    above = jnp.where(odd_strip, near, far)
    below = jnp.where(odd_strip, far, near)
    stack = [beneath]
    stack += [tiles_of(density_ref[p].astype(f32)) for p in range(planes)]
    stack += [overhead]
    table = [
        jnp.broadcast_to(table_ref[c : c + 1, :], (height, LANES)) for c in range(4)
    ]
    table[0] = table[0] * (LOG2E / total_planes)

    depth = [jnp.zeros((height, LANES), f32)] * count
    colour = [[jnp.zeros((height, LANES), f32)] * count for _ in range(3)]
    for p in range(planes):
        plane_index = brick * planes + p
        shift = (3 * plane_index) // 8
        fraction = ((3 * plane_index) % 8).astype(f32) / 8.0
        centre = stack[p + 1]
        ahead, behind = lane_next(centre, lane), lane_previous(centre, lane)
        fields = [[], [], [], []]
        for t in range(count):
            cols = slice(t * LANES, (t + 1) * LANES)
            v = centre[t]
            up = jnp.where(row == 0, above[p : p + 1, cols], pltpu.roll(v, 1, 0))
            down = jnp.where(
                row == height - 1, below[p : p + 1, cols], pltpu.roll(v, height - 1, 0)
            )
            dx = ahead[t] - behind[t]
            dy = down - up
            dz = stack[p + 2][t] - stack[p][t]
            gain = SHADE_GAIN * LOG2E
            lit = (LIGHT[0] * gain) * dx + (LIGHT[1] * gain) * dy + (LIGHT[2] * gain) * dz
            shade = jnp.exp2(lit * lax.rsqrt(4.0 + dx * dx + dy * dy + dz * dz))
            bins = bins_ref[p, :, cols]
            looked = [
                jnp.take_along_axis(entry, bins, axis=1, mode="promise_in_bounds")
                for entry in table
            ]
            extinction = looked[0] * (1.0 + v * v)
            strength = (1.0 - jnp.exp2(-extinction)) * shade
            fields[0].append(extinction)
            for c in range(3):
                fields[c + 1].append(looked[c + 1] * strength)
        sheared = []
        for field in fields:
            first = lane_shift(field, lane, shift)
            second = lane_next(first, lane)
            sheared.append([a + fraction * (b - a) for a, b in zip(first, second)])
        for t in range(count):
            through = jnp.exp2(-depth[t])
            for c in range(3):
                colour[c][t] = colour[c][t] + through * sheared[c + 1][t]
            depth[t] = depth[t] + sheared[0][t]

    depth_factor = CODE_MAX / depth_scale(planes, total_planes)
    words = [[], []]
    for t in range(count):
        codes = [jnp.minimum(depth[t] * depth_factor, CODE_MAX)]
        for c in range(3):
            code = jnp.log2(colour[c][t]) * COLOUR_STEPS - COLOUR_LOW * COLOUR_STEPS
            codes.append(jnp.minimum(jnp.maximum(code, 0.0), CODE_MAX))
        codes = [(code + 0.5).astype(jnp.int32) for code in codes]
        words[0].append(codes[0] | (codes[1] << 16))
        words[1].append(codes[2] | (codes[3] << 16))
    owned = height * across // bricks
    tall, wide = max(owned // across, 1), min(owned, across)
    for owner in range(bricks):
        top, left = owner * owned // across, owner * owned % across
        for w in range(2):
            for t in range(wide // LANES):
                out_ref[owner, w, t * tall : (t + 1) * tall, :] = words[w][left // LANES + t][
                    top : top + tall, :
                ]


def merge_kernel(planes, tall, order_ref, words_ref, out_ref):
    bricks, _, rows, _ = words_ref.shape
    f32 = jnp.float32
    depth_unit = depth_scale(planes, planes * bricks) / CODE_MAX
    passed = jnp.zeros((rows, LANES), f32)
    colour = [jnp.zeros((rows, LANES), f32)] * 3
    for k in range(bricks):
        brick = order_ref[0, k]
        words = [words_ref[brick, 0], words_ref[brick, 1]]
        codes = []
        for word in words:
            codes += [word & 0xFFFF, lax.shift_right_logical(word, 16)]
        base = COLOUR_LOW - passed
        for c in range(3):
            code = codes[c + 1]
            term = jnp.exp2(code.astype(f32) * (1.0 / COLOUR_STEPS) + base)
            colour[c] = colour[c] + jnp.where(code > 0, term, 0.0)
        passed = passed + codes[0].astype(f32) * depth_unit
    image = colour + [jnp.exp2(-passed)]
    wide = rows // tall
    for c in range(4):
        for r in range(tall):
            for t in range(wide):
                at = (r * wide + t) * LANES
                out_ref[c : c + 1, at : at + LANES] = image[c][t * tall + r : t * tall + r + 1, :]


def per_device(density, tf_bins, tf_table, brick_order):
    planes, height, across = density.shape
    bricks = lax.axis_size("depth")
    plane_near, plane_far = exchange(density, "depth", 0)
    row_near, row_far = exchange(density, "strip", 1)
    owned = height * across // bricks
    table = jnp.pad(tf_table, ((0, 0), (0, LANES - tf_table.shape[1])))
    vmem = pl.BlockSpec(memory_space=pltpu.VMEM)
    words = pl.pallas_call(
        functools.partial(brick_kernel, bricks),
        out_shape=jax.ShapeDtypeStruct((bricks, 2, owned // LANES, LANES), jnp.int32),
        in_specs=[vmem] * 7,
        out_specs=vmem,
        compiler_params=pltpu.CompilerParams(vmem_limit_bytes=VMEM_BYTES),
    )(density, tf_bins, table, plane_near, plane_far, row_near, row_far)
    words = lax.all_to_all(words, "depth", 0, 0, tiled=True)
    return pl.pallas_call(
        functools.partial(merge_kernel, planes, max(owned // across, 1)),
        out_shape=jax.ShapeDtypeStruct((4, owned), jnp.float32),
        in_specs=[pl.BlockSpec(memory_space=pltpu.SMEM), vmem],
        out_specs=vmem,
        compiler_params=pltpu.CompilerParams(vmem_limit_bytes=VMEM_BYTES),
    )(brick_order, words)


def solution(mesh):
    in_specs = (P("depth", "strip", None), P("depth", "strip", None), P(), P("strip", None))
    out_specs = P(None, ("strip", "depth"))
    return jax.shard_map(
        per_device, mesh=mesh, in_specs=in_specs, out_specs=out_specs, check_vma=False
    )
```

```python
import functools

import jax
import jax.numpy as jnp
from jax import lax
from jax.experimental import pallas as pl
from jax.experimental.pallas import tpu as pltpu
from jax.sharding import PartitionSpec as P

LIGHT = (0.36, 0.48, 0.8)
SHADE_GAIN = 1.5
LOG2E = 1.4426950408889634
LANES = 128
VMEM_BYTES = 8 * 1024 * 1024

MAX_DENSITY = 6.0
MAX_LOOKED = 2.0

COLOUR_STEPS = 2048.0
COLOUR_LOW = -28.0
CODE_MAX = 65535.0


def depth_scale(planes, total_planes):
    return MAX_LOOKED * (1.0 + MAX_DENSITY * MAX_DENSITY) * LOG2E * planes / total_planes


def pairs(count, start):
    swaps = []
    for i in range(start, count - 1, 2):
        swaps += [(i, i + 1), (i + 1, i)]
    return swaps


def edges_kernel(density_ref, plane_near, plane_far, row_near, row_far):
    planes, height, _ = density_ref.shape
    odd_brick = lax.axis_index("depth") % 2
    odd_strip = lax.axis_index("strip") % 2 == 1
    plane_near[...] = density_ref[pl.ds((1 - odd_brick) * (planes - 1), 1)]
    plane_far[...] = density_ref[pl.ds(odd_brick * (planes - 1), 1)]
    head, tail = density_ref[:, 0, :], density_ref[:, height - 1, :]
    row_near[:, 0, :] = jnp.where(odd_strip, head, tail)
    row_far[:, 0, :] = jnp.where(odd_strip, tail, head)


def swap(cells, axis, start):
    return lax.ppermute(cells, axis, pairs(lax.axis_size(axis), start))


def tiles_of(value):
    return [value[:, t : t + LANES] for t in range(0, value.shape[1], LANES)]


def lane_next(tiles, lane):
    rolled = [pltpu.roll(v, LANES - 1, 1) for v in tiles] + [0.0]
    return [jnp.where(lane < LANES - 1, rolled[t], rolled[t + 1]) for t in range(len(tiles))]


def lane_previous(tiles, lane):
    rolled = [0.0] + [pltpu.roll(v, 1, 1) for v in tiles]
    return [jnp.where(lane > 0, rolled[t + 1], rolled[t]) for t in range(len(tiles))]


def lane_shift(tiles, lane, shift, beyond):
    amount = (LANES - shift) % LANES
    rolled = [pltpu.roll(v, amount, 1) for v in tiles] + [beyond]
    return [jnp.where(lane < LANES - shift, rolled[t], rolled[t + 1]) for t in range(len(tiles))]


def light_kernel(
    bricks,
    density_ref,
    bins_ref,
    table_ref,
    order_ref,
    first_ref,
    second_ref,
    depth_ref,
    before_ref,
):
    planes, height, across = density_ref.shape
    total_planes = planes * bricks
    count = across // LANES
    f32 = jnp.float32
    lane = lax.broadcasted_iota(jnp.int32, (height, LANES), 1)
    table = [jnp.broadcast_to(table_ref[c : c + 1, :], (height, LANES)) for c in range(4)]
    table[0] = table[0] * (LOG2E / total_planes)
    depth = [jnp.zeros((height, LANES), f32)] * count
    for p in range(planes):
        plane_index = lax.axis_index("depth") * planes + p
        shift = (3 * plane_index) // 8
        fraction = ((3 * plane_index) % 8).astype(f32) / 8.0
        cells = lane_shift(tiles_of(density_ref[p].astype(f32)), lane, shift, 0.0)
        bins = lane_shift(tiles_of(bins_ref[p]), lane, shift, LANES - 1)
        fields = [[], [], [], []]
        for t in range(count):
            looked = [
                jnp.take_along_axis(entry, bins[t], axis=1, mode="promise_in_bounds")
                for entry in table
            ]
            extinction = looked[0] * (1.0 + cells[t] * cells[t])
            opacity = 1.0 - jnp.exp2(-extinction)
            fields[0].append(extinction)
            for c in range(3):
                fields[c + 1].append(looked[c + 1] * opacity)
        after = [lane_next(field, lane) for field in fields]
        for t in range(count):
            cols = slice(t * LANES, (t + 1) * LANES)
            through = jnp.exp2(-depth[t])
            through_second = through * fraction
            through_first = through - through_second
            for c in range(3):
                first_ref[p, c, :, cols] = through_first * fields[c + 1][t]
                second_ref[p, c, :, cols] = through_second * after[c + 1][t]
            depth[t] = depth[t] + (
                fields[0][t] + fraction * (after[0][t] - fields[0][t])
            )
    depth_factor = CODE_MAX / depth_scale(planes, total_planes)
    for t in range(count):
        code = jnp.minimum(depth[t] * depth_factor, CODE_MAX)
        depth_ref[:, t * LANES : (t + 1) * LANES] = (code + 0.5).astype(jnp.int32)
    slot = lax.broadcasted_iota(jnp.int32, (bricks, LANES), 0)
    place = jnp.zeros((bricks, LANES), jnp.int32)
    for k in range(bricks):
        place = jnp.where(slot == order_ref[0, k], k, place)
    for b in range(bricks):
        before_ref[b] = (place < place[b : b + 1, :]).astype(f32)


def shade_kernel(
    bricks,
    plane_far,
    plane_near,
    row_near,
    row_far,
    density_ref,
    first_ref,
    second_ref,
    depth_ref,
    out_ref,
):
    planes, height, across = density_ref.shape
    count = across // LANES
    f32 = jnp.float32
    odd_brick = lax.axis_index("depth") % 2 == 1
    odd_strip = lax.axis_index("strip") % 2 == 1
    lane = lax.broadcasted_iota(jnp.int32, (height, LANES), 1)
    row = lax.broadcasted_iota(jnp.int32, (height, LANES), 0)
    near, far = plane_near[0].astype(f32), plane_far[0].astype(f32)
    beneath = tiles_of(jnp.where(odd_brick, near, far))
    overhead = tiles_of(jnp.where(odd_brick, far, near))
    near, far = row_near[:, 0, :].astype(f32), row_far[:, 0, :].astype(f32)
    above = jnp.where(odd_strip, near, far)
    below = jnp.where(odd_strip, far, near)
    stack = [beneath]
    stack += [tiles_of(density_ref[p].astype(f32)) for p in range(planes)]
    stack += [overhead]
    gain = SHADE_GAIN * LOG2E
    colour = [[None] * count for _ in range(3)]
    for p in range(planes):
        shift = (3 * (lax.axis_index("depth") * planes + p)) // 8
        centre = stack[p + 1]
        ahead, behind = lane_next(centre, lane), lane_previous(centre, lane)
        shade = []
        for t in range(count):
            cols = slice(t * LANES, (t + 1) * LANES)
            v = centre[t]
            up = jnp.where(row == 0, above[p : p + 1, cols], pltpu.roll(v, 1, 0))
            down = jnp.where(
                row == height - 1, below[p : p + 1, cols], pltpu.roll(v, height - 1, 0)
            )
            dx = ahead[t] - behind[t]
            dy = down - up
            dz = stack[p + 2][t] - stack[p][t]
            lit = (LIGHT[0] * gain) * dx + (LIGHT[1] * gain) * dy + (LIGHT[2] * gain) * dz
            shade.append(jnp.exp2(lit * lax.rsqrt(4.0 + dx * dx + dy * dy + dz * dz)))
        shade = lane_shift(shade, lane, shift, 0.0)
        after = lane_next(shade, lane)
        for t in range(count):
            cols = slice(t * LANES, (t + 1) * LANES)
            for c in range(3):
                term = first_ref[p, c, :, cols] * shade[t] + second_ref[p, c, :, cols] * after[t]
                colour[c][t] = term if p == 0 else colour[c][t] + term

    words = [[], []]
    for t in range(count):
        codes = [depth_ref[:, t * LANES : (t + 1) * LANES]]
        for c in range(3):
            code = jnp.log2(colour[c][t]) * COLOUR_STEPS + (0.5 - COLOUR_LOW * COLOUR_STEPS)
            codes.append(jnp.minimum(jnp.maximum(code, 0.0), CODE_MAX).astype(jnp.int32))
        words[0].append(codes[0] | (codes[1] << 16))
        words[1].append(codes[2] | (codes[3] << 16))
    owned = height * across // bricks
    tall, wide = max(owned // across, 1), min(owned, across)
    for owner in range(bricks):
        top, left = owner * owned // across, owner * owned % across
        for w in range(2):
            for t in range(wide // LANES):
                out_ref[owner, w, t * tall : (t + 1) * tall, :] = words[w][left // LANES + t][
                    top : top + tall, :
                ]


def merge_kernel(planes, tall, before_ref, words_ref, out_ref):
    bricks, _, rows, _ = words_ref.shape
    f32 = jnp.float32
    depth_unit = depth_scale(planes, planes * bricks) / CODE_MAX
    depth, codes = [], []
    for b in range(bricks):
        low, high = words_ref[b, 0], words_ref[b, 1]
        depth.append((low & 0xFFFF).astype(f32) * depth_unit)
        codes.append(
            [lax.shift_right_logical(low, 16), high & 0xFFFF, lax.shift_right_logical(high, 16)]
        )
    colour = [jnp.zeros((rows, LANES), f32)] * 3
    for b in range(bricks):
        base = jnp.full((rows, LANES), COLOUR_LOW, f32)
        for other in range(bricks):
            if other != b:
                base = base - before_ref[b, other : other + 1, :] * depth[other]
        for c in range(3):
            term = jnp.exp2(codes[b][c].astype(f32) * (1.0 / COLOUR_STEPS) + base)
            colour[c] = colour[c] + jnp.where(codes[b][c] > 0, term, 0.0)
    image = colour + [jnp.exp2(-sum(depth))]
    wide = rows // tall
    for c in range(4):
        for r in range(tall):
            for t in range(wide):
                at = (r * wide + t) * LANES
                out_ref[c : c + 1, at : at + LANES] = image[c][t * tall + r : t * tall + r + 1, :]


def call(kernel, out_shape, *operands, scalars=()):
    vmem = pl.BlockSpec(memory_space=pltpu.VMEM)
    smem = pl.BlockSpec(memory_space=pltpu.SMEM)
    return pl.pallas_call(
        kernel,
        out_shape=out_shape,
        in_specs=[smem if i in scalars else vmem for i in range(len(operands))],
        out_specs=jax.tree.map(lambda _: vmem, out_shape),
        compiler_params=pltpu.CompilerParams(vmem_limit_bytes=VMEM_BYTES),
    )(*operands)


def per_device(density, tf_bins, tf_table, brick_order):
    planes, height, across = density.shape
    bricks = lax.axis_size("depth")
    owned = height * across // bricks
    shape = jax.ShapeDtypeStruct
    table = jnp.pad(tf_table, ((0, 0), (0, LANES - tf_table.shape[1])))
    plane = shape((1, height, across), density.dtype)
    rows = shape((planes, 1, across), density.dtype)
    plane_near, plane_far, row_near, row_far = call(
        edges_kernel, [plane, plane, rows, rows], density
    )
    plane_far = swap(plane_far, "depth", 1)
    plane_near = swap(plane_near, "depth", 0)
    row_near = swap(row_near, "strip", 0)
    row_far = swap(row_far, "strip", 1)
    sheared = shape((planes, 3, height, across), jnp.float32)
    first, second, depth, before = call(
        functools.partial(light_kernel, bricks),
        [
            sheared,
            sheared,
            shape((height, across), jnp.int32),
            shape((bricks, bricks, LANES), jnp.float32),
        ],
        density,
        tf_bins,
        table,
        brick_order,
        scalars=(3,),
    )
    words = call(
        functools.partial(shade_kernel, bricks),
        shape((bricks, 2, owned // LANES, LANES), jnp.int32),
        plane_far,
        plane_near,
        row_near,
        row_far,
        density,
        first,
        second,
        depth,
    )
    words = lax.all_to_all(words, "depth", 0, 0, tiled=True)
    return call(
        functools.partial(merge_kernel, planes, max(owned // across, 1)),
        shape((4, owned), jnp.float32),
        before,
        words,
    )


def solution(mesh):
    in_specs = (P("depth", "strip", None), P("depth", "strip", None), P(), P("strip", None))
    out_specs = P(None, ("strip", "depth"))
    return jax.shard_map(
        per_device, mesh=mesh, in_specs=in_specs, out_specs=out_specs, check_vma=False
    )
```

```python
import functools

import jax
import jax.numpy as jnp
from jax import lax
from jax.experimental import pallas as pl
from jax.experimental.pallas import tpu as pltpu
from jax.sharding import PartitionSpec as P

LIGHT = (0.36, 0.48, 0.8)
SHADE_GAIN = 1.5
LOG2E = 1.4426950408889634
LANES = 128
VMEM_BYTES = 8 * 1024 * 1024

MAX_DENSITY = 6.0
MAX_LOOKED = 2.0

COLOUR_STEPS = 2048.0
COLOUR_LOW = -28.0
CODE_MAX = 65535.0


def depth_scale(planes, total_planes):
    return MAX_LOOKED * (1.0 + MAX_DENSITY * MAX_DENSITY) * LOG2E * planes / total_planes


def pairs(count, start):
    swaps = []
    for i in range(start, count - 1, 2):
        swaps += [(i, i + 1), (i + 1, i)]
    return swaps


def edges_kernel(
    density_hbm,
    bins_hbm,
    table_hbm,
    order_hbm,
    density_ref,
    bins_ref,
    table_ref,
    order_ref,
    plane_near,
    plane_far,
    row_near,
    row_far,
    small_ref,
    semaphores,
):
    density_copy = pltpu.make_async_copy(density_hbm, density_ref, semaphores.at[0])
    bins_copy = pltpu.make_async_copy(bins_hbm, bins_ref, semaphores.at[1])
    density_copy.start()
    bins_copy.start()
    table_copy = pltpu.make_async_copy(table_hbm, small_ref, semaphores.at[2])
    order_copy = pltpu.make_async_copy(order_hbm, order_ref, semaphores.at[3])
    table_copy.start()
    order_copy.start()
    table_ref[...] = jnp.zeros_like(table_ref)
    planes, height, _ = density_ref.shape
    odd_brick = lax.axis_index("depth") % 2
    odd_strip = lax.axis_index("strip") % 2 == 1
    density_copy.wait()
    plane_near[...] = density_ref[pl.ds((1 - odd_brick) * (planes - 1), 1)]
    plane_far[...] = density_ref[pl.ds(odd_brick * (planes - 1), 1)]
    head, tail = density_ref[:, 0, :], density_ref[:, height - 1, :]
    row_near[:, 0, :] = jnp.where(odd_strip, head, tail)
    row_far[:, 0, :] = jnp.where(odd_strip, tail, head)
    table_copy.wait()
    table_ref[:, : small_ref.shape[1]] = small_ref[...]
    order_copy.wait()
    bins_copy.wait()


def swap(cells, axis, start):
    return lax.ppermute(cells, axis, pairs(lax.axis_size(axis), start))


def tiles_of(value):
    return [value[:, t : t + LANES] for t in range(0, value.shape[1], LANES)]


def lane_next(tiles, lane):
    rolled = [pltpu.roll(v, LANES - 1, 1) for v in tiles] + [0.0]
    return [jnp.where(lane < LANES - 1, rolled[t], rolled[t + 1]) for t in range(len(tiles))]


def lane_previous(tiles, lane):
    rolled = [0.0] + [pltpu.roll(v, 1, 1) for v in tiles]
    return [jnp.where(lane > 0, rolled[t + 1], rolled[t]) for t in range(len(tiles))]


def lane_shift(tiles, lane, shift, beyond):
    amount = (LANES - shift) % LANES
    rolled = [pltpu.roll(v, amount, 1) for v in tiles] + [beyond]
    return [jnp.where(lane < LANES - shift, rolled[t], rolled[t + 1]) for t in range(len(tiles))]


def light_kernel(
    bricks,
    density_ref,
    bins_ref,
    table_ref,
    order_ref,
    first_ref,
    second_ref,
    depth_ref,
    before_ref,
):
    planes, height, across = density_ref.shape
    total_planes = planes * bricks
    count = across // LANES
    f32 = jnp.float32
    lane = lax.broadcasted_iota(jnp.int32, (height, LANES), 1)
    table = [jnp.broadcast_to(table_ref[c : c + 1, :], (height, LANES)) for c in range(4)]
    table[0] = table[0] * (LOG2E / total_planes)
    depth = [jnp.zeros((height, LANES), f32)] * count
    for p in range(planes):
        plane_index = lax.axis_index("depth") * planes + p
        shift = (3 * plane_index) // 8
        fraction = ((3 * plane_index) % 8).astype(f32) / 8.0
        cells = lane_shift(tiles_of(density_ref[p].astype(f32)), lane, shift, 0.0)
        bins = lane_shift(tiles_of(bins_ref[p]), lane, shift, LANES - 1)
        fields = [[], [], [], []]
        for t in range(count):
            looked = [
                jnp.take_along_axis(entry, bins[t], axis=1, mode="promise_in_bounds")
                for entry in table
            ]
            extinction = looked[0] * (1.0 + cells[t] * cells[t])
            opacity = 1.0 - jnp.exp2(-extinction)
            fields[0].append(extinction)
            for c in range(3):
                fields[c + 1].append(looked[c + 1] * opacity)
        after = [lane_next(field, lane) for field in fields]
        for t in range(count):
            cols = slice(t * LANES, (t + 1) * LANES)
            through = jnp.exp2(-depth[t])
            through_second = through * fraction
            through_first = through - through_second
            for c in range(3):
                first_ref[p, c, :, cols] = through_first * fields[c + 1][t]
                second_ref[p, c, :, cols] = through_second * after[c + 1][t]
            depth[t] = depth[t] + (
                fields[0][t] + fraction * (after[0][t] - fields[0][t])
            )
    depth_factor = CODE_MAX / depth_scale(planes, total_planes)
    for t in range(count):
        code = jnp.minimum(depth[t] * depth_factor, CODE_MAX)
        depth_ref[:, t * LANES : (t + 1) * LANES] = (code + 0.5).astype(jnp.int32)
    slot = lax.broadcasted_iota(jnp.int32, (bricks, LANES), 0)
    place = jnp.zeros((bricks, LANES), jnp.int32)
    for k in range(bricks):
        brick = jnp.broadcast_to(order_ref[0:1, k : k + 1], (bricks, LANES))
        place = jnp.where(slot == brick, k, place)
    for b in range(bricks):
        before_ref[b] = (place < place[b : b + 1, :]).astype(f32)


def shade_kernel(
    bricks,
    plane_far,
    plane_near,
    row_near,
    row_far,
    density_ref,
    first_ref,
    second_ref,
    depth_ref,
    out_ref,
):
    planes, height, across = density_ref.shape
    count = across // LANES
    f32 = jnp.float32
    odd_brick = lax.axis_index("depth") % 2 == 1
    odd_strip = lax.axis_index("strip") % 2 == 1
    lane = lax.broadcasted_iota(jnp.int32, (height, LANES), 1)
    row = lax.broadcasted_iota(jnp.int32, (height, LANES), 0)
    near, far = plane_near[0].astype(f32), plane_far[0].astype(f32)
    beneath = tiles_of(jnp.where(odd_brick, near, far))
    overhead = tiles_of(jnp.where(odd_brick, far, near))
    near, far = row_near[:, 0, :].astype(f32), row_far[:, 0, :].astype(f32)
    above = jnp.where(odd_strip, near, far)
    below = jnp.where(odd_strip, far, near)
    stack = [beneath]
    stack += [tiles_of(density_ref[p].astype(f32)) for p in range(planes)]
    stack += [overhead]
    gain = SHADE_GAIN * LOG2E
    colour = [[None] * count for _ in range(3)]
    for p in range(planes):
        shift = (3 * (lax.axis_index("depth") * planes + p)) // 8
        centre = stack[p + 1]
        ahead, behind = lane_next(centre, lane), lane_previous(centre, lane)
        shade = []
        for t in range(count):
            cols = slice(t * LANES, (t + 1) * LANES)
            v = centre[t]
            up = jnp.where(row == 0, above[p : p + 1, cols], pltpu.roll(v, 1, 0))
            down = jnp.where(
                row == height - 1, below[p : p + 1, cols], pltpu.roll(v, height - 1, 0)
            )
            dx = ahead[t] - behind[t]
            dy = down - up
            dz = stack[p + 2][t] - stack[p][t]
            lit = (LIGHT[0] * gain) * dx + (LIGHT[1] * gain) * dy + (LIGHT[2] * gain) * dz
            shade.append(jnp.exp2(lit * lax.rsqrt(4.0 + dx * dx + dy * dy + dz * dz)))
        shade = lane_shift(shade, lane, shift, 0.0)
        after = lane_next(shade, lane)
        for t in range(count):
            cols = slice(t * LANES, (t + 1) * LANES)
            for c in range(3):
                term = first_ref[p, c, :, cols] * shade[t] + second_ref[p, c, :, cols] * after[t]
                colour[c][t] = term if p == 0 else colour[c][t] + term

    words = [[], []]
    for t in range(count):
        codes = [depth_ref[:, t * LANES : (t + 1) * LANES]]
        for c in range(3):
            code = jnp.log2(colour[c][t]) * COLOUR_STEPS + (0.5 - COLOUR_LOW * COLOUR_STEPS)
            codes.append(jnp.minimum(jnp.maximum(code, 0.0), CODE_MAX).astype(jnp.int32))
        words[0].append(codes[0] | (codes[1] << 16))
        words[1].append(codes[2] | (codes[3] << 16))
    owned = height * across // bricks
    tall, wide = max(owned // across, 1), min(owned, across)
    for owner in range(bricks):
        top, left = owner * owned // across, owner * owned % across
        for w in range(2):
            for t in range(wide // LANES):
                out_ref[owner, w, t * tall : (t + 1) * tall, :] = words[w][left // LANES + t][
                    top : top + tall, :
                ]


def merge_kernel(planes, tall, before_ref, words_ref, out_ref):
    bricks, _, rows, _ = words_ref.shape
    f32 = jnp.float32
    depth_unit = depth_scale(planes, planes * bricks) / CODE_MAX
    depth, codes = [], []
    for b in range(bricks):
        low, high = words_ref[b, 0], words_ref[b, 1]
        depth.append((low & 0xFFFF).astype(f32) * depth_unit)
        codes.append(
            [lax.shift_right_logical(low, 16), high & 0xFFFF, lax.shift_right_logical(high, 16)]
        )
    colour = [jnp.zeros((rows, LANES), f32)] * 3
    for b in range(bricks):
        base = jnp.full((rows, LANES), COLOUR_LOW, f32)
        for other in range(bricks):
            if other != b:
                base = base - before_ref[b, other : other + 1, :] * depth[other]
        for c in range(3):
            term = jnp.exp2(codes[b][c].astype(f32) * (1.0 / COLOUR_STEPS) + base)
            colour[c] = colour[c] + jnp.where(codes[b][c] > 0, term, 0.0)
    image = colour + [jnp.exp2(-sum(depth))]
    wide = rows // tall
    for c in range(4):
        for r in range(tall):
            for t in range(wide):
                at = (r * wide + t) * LANES
                out_ref[c : c + 1, at : at + LANES] = image[c][t * tall + r : t * tall + r + 1, :]


def call(kernel, out_shape, *operands, spaces=None, scratch=()):
    vmem = pl.BlockSpec(memory_space=pltpu.VMEM)
    spaces = spaces or {}
    return pl.pallas_call(
        kernel,
        out_shape=out_shape,
        in_specs=[
            pl.BlockSpec(memory_space=spaces.get(i, pltpu.VMEM)) for i in range(len(operands))
        ],
        out_specs=jax.tree.map(lambda _: vmem, out_shape),
        scratch_shapes=scratch,
        compiler_params=pltpu.CompilerParams(vmem_limit_bytes=VMEM_BYTES),
    )(*operands)


def per_device(density, tf_bins, tf_table, brick_order):
    planes, height, across = density.shape
    bricks = lax.axis_size("depth")
    owned = height * across // bricks
    shape = jax.ShapeDtypeStruct
    plane = shape((1, height, across), density.dtype)
    rows = shape((planes, 1, across), density.dtype)
    density, tf_bins, table, order, plane_near, plane_far, row_near, row_far = call(
        edges_kernel,
        [
            shape(density.shape, density.dtype),
            shape(tf_bins.shape, tf_bins.dtype),
            shape((tf_table.shape[0], LANES), tf_table.dtype),
            shape(brick_order.shape, brick_order.dtype),
            plane,
            plane,
            rows,
            rows,
        ],
        *[
            pltpu.with_memory_space_constraint(argument, pltpu.HBM)
            for argument in (density, tf_bins, tf_table, brick_order)
        ],
        spaces={i: pltpu.HBM for i in range(4)},
        scratch=[pltpu.VMEM(tf_table.shape, tf_table.dtype), pltpu.SemaphoreType.DMA((4,))],
    )
    plane_far = swap(plane_far, "depth", 1)
    plane_near = swap(plane_near, "depth", 0)
    row_near = swap(row_near, "strip", 0)
    row_far = swap(row_far, "strip", 1)
    sheared = shape((planes, 3, height, across), jnp.float32)
    first, second, depth, before = call(
        functools.partial(light_kernel, bricks),
        [
            sheared,
            sheared,
            shape((height, across), jnp.int32),
            shape((bricks, bricks, LANES), jnp.float32),
        ],
        density,
        tf_bins,
        table,
        order,
    )
    words = call(
        functools.partial(shade_kernel, bricks),
        shape((bricks, 2, owned // LANES, LANES), jnp.int32),
        plane_far,
        plane_near,
        row_near,
        row_far,
        density,
        first,
        second,
        depth,
    )
    words = lax.all_to_all(words, "depth", 0, 0, tiled=True)
    return call(
        functools.partial(merge_kernel, planes, max(owned // across, 1)),
        shape((4, owned), jnp.float32),
        before,
        words,
    )


def solution(mesh):
    in_specs = (P("depth", "strip", None), P("depth", "strip", None), P(), P("strip", None))
    out_specs = P(None, ("strip", "depth"))
    return jax.shard_map(
        per_device, mesh=mesh, in_specs=in_specs, out_specs=out_specs, check_vma=False
    )
```

```python
import functools

import jax
import jax.numpy as jnp
from jax import lax
from jax.experimental import pallas as pl
from jax.experimental.pallas import tpu as pltpu
from jax.sharding import PartitionSpec as P

LIGHT = (0.36, 0.48, 0.8)
SHADE_GAIN = 1.5
LOG2E = 1.4426950408889634
LANES = 128
VMEM_BYTES = 8 * 1024 * 1024

MAX_DENSITY = 6.0
MAX_LOOKED = 2.0

COLOUR_STEPS = 2048.0
COLOUR_LOW = -28.0
CODE_MAX = 65535.0


def depth_scale(planes, total_planes):
    return MAX_LOOKED * (1.0 + MAX_DENSITY * MAX_DENSITY) * LOG2E * planes / total_planes


def pairs(count, start):
    swaps = []
    for i in range(start, count - 1, 2):
        swaps += [(i, i + 1), (i + 1, i)]
    return swaps


def partner_exists(index, count, start):
    lower = index % 2 == start
    return jnp.where(lower, index + 1 < count, index > 0)


def edges_kernel(
    density_hbm,
    bins_hbm,
    table_hbm,
    order_hbm,
    density_ref,
    bins_ref,
    table_ref,
    order_ref,
    plane_near,
    plane_far,
    row_near,
    row_far,
    small_ref,
    semaphores,
):
    density_copy = pltpu.make_async_copy(density_hbm, density_ref, semaphores.at[0])
    bins_copy = pltpu.make_async_copy(bins_hbm, bins_ref, semaphores.at[1])
    density_copy.start()
    bins_copy.start()
    table_copy = pltpu.make_async_copy(table_hbm, small_ref, semaphores.at[2])
    order_copy = pltpu.make_async_copy(order_hbm, order_ref, semaphores.at[3])
    table_copy.start()
    order_copy.start()
    table_ref[...] = jnp.zeros_like(table_ref)
    planes, height, _ = density_ref.shape
    odd_brick = lax.axis_index("depth") % 2
    odd_strip = lax.axis_index("strip") % 2 == 1
    density_copy.wait()
    plane_near[...] = density_ref[pl.ds((1 - odd_brick) * (planes - 1), 1)]
    plane_far[...] = density_ref[pl.ds(odd_brick * (planes - 1), 1)]
    head, tail = density_ref[:, 0, :], density_ref[:, height - 1, :]
    row_near[:, 0, :] = jnp.where(odd_strip, head, tail)
    row_far[:, 0, :] = jnp.where(odd_strip, tail, head)
    table_copy.wait()
    table_ref[:, : small_ref.shape[1]] = small_ref[...]
    order_copy.wait()
    bins_copy.wait()


def swap(cells, axis, start):
    bricks, strips = lax.axis_size("depth"), lax.axis_size("strip")
    count = bricks if axis == "depth" else strips
    swaps = pairs(count, start)
    spare = [i for i in range(count) if (i, i + 1) not in swaps and (i, i - 1) not in swaps]
    if axis == "depth":
        links = [((a, s), (b, s)) for a, b in swaps for s in range(strips)]
        if strips % 2 == 0:
            links += [((a, s), (a, s ^ 1)) for a in spare for s in range(strips)]
    else:
        if len(spare) == 2:
            swaps = swaps + [tuple(spare), tuple(spare[::-1])]
        links = [((d, a), (d, b)) for a, b in swaps for d in range(bricks)]
    flat = [(a * strips + s, b * strips + t) for (a, s), (b, t) in links]
    return lax.ppermute(cells, ("depth", "strip"), flat)


def masked(cells, axis, start):
    exists = partner_exists(lax.axis_index(axis), lax.axis_size(axis), start)
    return jnp.where(exists, cells, 0.0)


def tiles_of(value):
    return [value[:, t : t + LANES] for t in range(0, value.shape[1], LANES)]


def lane_next(tiles, lane):
    rolled = [pltpu.roll(v, LANES - 1, 1) for v in tiles] + [0.0]
    return [jnp.where(lane < LANES - 1, rolled[t], rolled[t + 1]) for t in range(len(tiles))]


def lane_previous(tiles, lane):
    rolled = [0.0] + [pltpu.roll(v, 1, 1) for v in tiles]
    return [jnp.where(lane > 0, rolled[t + 1], rolled[t]) for t in range(len(tiles))]


def lane_shift(tiles, lane, shift, beyond):
    amount = (LANES - shift) % LANES
    rolled = [pltpu.roll(v, amount, 1) for v in tiles] + [beyond]
    return [jnp.where(lane < LANES - shift, rolled[t], rolled[t + 1]) for t in range(len(tiles))]


def light_kernel(
    bricks,
    density_ref,
    bins_ref,
    table_ref,
    order_ref,
    first_ref,
    second_ref,
    depth_ref,
    before_ref,
):
    planes, height, across = density_ref.shape
    total_planes = planes * bricks
    count = across // LANES
    f32 = jnp.float32
    lane = lax.broadcasted_iota(jnp.int32, (height, LANES), 1)
    table = [jnp.broadcast_to(table_ref[c : c + 1, :], (height, LANES)) for c in range(4)]
    table[0] = table[0] * (LOG2E / total_planes)
    depth = [jnp.zeros((height, LANES), f32)] * count
    for p in range(planes):
        plane_index = lax.axis_index("depth") * planes + p
        shift = (3 * plane_index) // 8
        fraction = ((3 * plane_index) % 8).astype(f32) / 8.0
        cells = lane_shift(tiles_of(density_ref[p].astype(f32)), lane, shift, 0.0)
        bins = lane_shift(tiles_of(bins_ref[p]), lane, shift, LANES - 1)
        fields = [[], [], [], []]
        for t in range(count):
            looked = [
                jnp.take_along_axis(entry, bins[t], axis=1, mode="promise_in_bounds")
                for entry in table
            ]
            extinction = looked[0] * (1.0 + cells[t] * cells[t])
            opacity = 1.0 - jnp.exp2(-extinction)
            fields[0].append(extinction)
            for c in range(3):
                fields[c + 1].append(looked[c + 1] * opacity)
        after = [lane_next(field, lane) for field in fields]
        for t in range(count):
            cols = slice(t * LANES, (t + 1) * LANES)
            through = jnp.exp2(-depth[t])
            through_second = through * fraction
            through_first = through - through_second
            for c in range(3):
                first_ref[p, c, :, cols] = through_first * fields[c + 1][t]
                second_ref[p, c, :, cols] = through_second * after[c + 1][t]
            depth[t] = depth[t] + (
                fields[0][t] + fraction * (after[0][t] - fields[0][t])
            )
    depth_factor = CODE_MAX / depth_scale(planes, total_planes)
    for t in range(count):
        code = jnp.minimum(depth[t] * depth_factor, CODE_MAX)
        depth_ref[:, t * LANES : (t + 1) * LANES] = (code + 0.5).astype(jnp.int32)
    slot = lax.broadcasted_iota(jnp.int32, (bricks, LANES), 0)
    place = jnp.zeros((bricks, LANES), jnp.int32)
    for k in range(bricks):
        brick = jnp.broadcast_to(order_ref[0:1, k : k + 1], (bricks, LANES))
        place = jnp.where(slot == brick, k, place)
    for b in range(bricks):
        before_ref[b] = (place < place[b : b + 1, :]).astype(f32)


def shade_kernel(
    bricks,
    plane_far,
    plane_near,
    row_near,
    row_far,
    density_ref,
    first_ref,
    second_ref,
    depth_ref,
    out_ref,
):
    planes, height, across = density_ref.shape
    count = across // LANES
    f32 = jnp.float32
    odd_brick = lax.axis_index("depth") % 2 == 1
    odd_strip = lax.axis_index("strip") % 2 == 1
    lane = lax.broadcasted_iota(jnp.int32, (height, LANES), 1)
    row = lax.broadcasted_iota(jnp.int32, (height, LANES), 0)
    near = masked(plane_near[0].astype(f32), "depth", 0)
    far = masked(plane_far[0].astype(f32), "depth", 1)
    beneath = tiles_of(jnp.where(odd_brick, near, far))
    overhead = tiles_of(jnp.where(odd_brick, far, near))
    near = masked(row_near[:, 0, :].astype(f32), "strip", 0)
    far = masked(row_far[:, 0, :].astype(f32), "strip", 1)
    above = jnp.where(odd_strip, near, far)
    below = jnp.where(odd_strip, far, near)
    stack = [beneath]
    stack += [tiles_of(density_ref[p].astype(f32)) for p in range(planes)]
    stack += [overhead]
    gain = SHADE_GAIN * LOG2E
    colour = [[None] * count for _ in range(3)]
    for p in range(planes):
        shift = (3 * (lax.axis_index("depth") * planes + p)) // 8
        centre = stack[p + 1]
        ahead, behind = lane_next(centre, lane), lane_previous(centre, lane)
        shade = []
        for t in range(count):
            cols = slice(t * LANES, (t + 1) * LANES)
            v = centre[t]
            up = jnp.where(row == 0, above[p : p + 1, cols], pltpu.roll(v, 1, 0))
            down = jnp.where(
                row == height - 1, below[p : p + 1, cols], pltpu.roll(v, height - 1, 0)
            )
            dx = ahead[t] - behind[t]
            dy = down - up
            dz = stack[p + 2][t] - stack[p][t]
            lit = (LIGHT[0] * gain) * dx + (LIGHT[1] * gain) * dy + (LIGHT[2] * gain) * dz
            shade.append(jnp.exp2(lit * lax.rsqrt(4.0 + dx * dx + dy * dy + dz * dz)))
        shade = lane_shift(shade, lane, shift, 0.0)
        after = lane_next(shade, lane)
        for t in range(count):
            cols = slice(t * LANES, (t + 1) * LANES)
            for c in range(3):
                term = first_ref[p, c, :, cols] * shade[t] + second_ref[p, c, :, cols] * after[t]
                colour[c][t] = term if p == 0 else colour[c][t] + term

    words = [[], []]
    for t in range(count):
        codes = [depth_ref[:, t * LANES : (t + 1) * LANES]]
        for c in range(3):
            code = jnp.log2(colour[c][t]) * COLOUR_STEPS + (0.5 - COLOUR_LOW * COLOUR_STEPS)
            codes.append(jnp.minimum(jnp.maximum(code, 0.0), CODE_MAX).astype(jnp.int32))
        words[0].append(codes[0] | (codes[1] << 16))
        words[1].append(codes[2] | (codes[3] << 16))
    owned = height * across // bricks
    tall, wide = max(owned // across, 1), min(owned, across)
    for owner in range(bricks):
        top, left = owner * owned // across, owner * owned % across
        for w in range(2):
            for t in range(wide // LANES):
                out_ref[owner, w, t * tall : (t + 1) * tall, :] = words[w][left // LANES + t][
                    top : top + tall, :
                ]


def merge_kernel(planes, tall, before_ref, words_ref, out_ref):
    bricks, _, rows, _ = words_ref.shape
    f32 = jnp.float32
    depth_unit = depth_scale(planes, planes * bricks) / CODE_MAX
    depth, codes = [], []
    for b in range(bricks):
        low, high = words_ref[b, 0], words_ref[b, 1]
        depth.append((low & 0xFFFF).astype(f32) * depth_unit)
        codes.append(
            [lax.shift_right_logical(low, 16), high & 0xFFFF, lax.shift_right_logical(high, 16)]
        )
    colour = [jnp.zeros((rows, LANES), f32)] * 3
    for b in range(bricks):
        base = jnp.full((rows, LANES), COLOUR_LOW, f32)
        for other in range(bricks):
            if other != b:
                base = base - before_ref[b, other : other + 1, :] * depth[other]
        for c in range(3):
            term = jnp.exp2(codes[b][c].astype(f32) * (1.0 / COLOUR_STEPS) + base)
            colour[c] = colour[c] + jnp.where(codes[b][c] > 0, term, 0.0)
    image = colour + [jnp.exp2(-sum(depth))]
    wide = rows // tall
    for c in range(4):
        for r in range(tall):
            for t in range(wide):
                at = (r * wide + t) * LANES
                out_ref[c : c + 1, at : at + LANES] = image[c][t * tall + r : t * tall + r + 1, :]


def call(kernel, out_shape, *operands, spaces=None, scratch=()):
    vmem = pl.BlockSpec(memory_space=pltpu.VMEM)
    spaces = spaces or {}
    return pl.pallas_call(
        kernel,
        out_shape=out_shape,
        in_specs=[
            pl.BlockSpec(memory_space=spaces.get(i, pltpu.VMEM)) for i in range(len(operands))
        ],
        out_specs=jax.tree.map(lambda _: vmem, out_shape),
        scratch_shapes=scratch,
        compiler_params=pltpu.CompilerParams(vmem_limit_bytes=VMEM_BYTES),
    )(*operands)


def per_device(density, tf_bins, tf_table, brick_order):
    planes, height, across = density.shape
    bricks = lax.axis_size("depth")
    owned = height * across // bricks
    shape = jax.ShapeDtypeStruct
    plane = shape((1, height, across), density.dtype)
    rows = shape((planes, 1, across), density.dtype)
    density, tf_bins, table, order, plane_near, plane_far, row_near, row_far = call(
        edges_kernel,
        [
            shape(density.shape, density.dtype),
            shape(tf_bins.shape, tf_bins.dtype),
            shape((tf_table.shape[0], LANES), tf_table.dtype),
            shape(brick_order.shape, brick_order.dtype),
            plane,
            plane,
            rows,
            rows,
        ],
        *[
            pltpu.with_memory_space_constraint(argument, pltpu.HBM)
            for argument in (density, tf_bins, tf_table, brick_order)
        ],
        spaces={i: pltpu.HBM for i in range(4)},
        scratch=[pltpu.VMEM(tf_table.shape, tf_table.dtype), pltpu.SemaphoreType.DMA((4,))],
    )
    plane_far = swap(plane_far, "depth", 1)
    plane_near = swap(plane_near, "depth", 0)
    row_near = swap(row_near, "strip", 0)
    row_far = swap(row_far, "strip", 1)
    sheared = shape((planes, 3, height, across), jnp.float32)
    first, second, depth, before = call(
        functools.partial(light_kernel, bricks),
        [
            sheared,
            sheared,
            shape((height, across), jnp.int32),
            shape((bricks, bricks, LANES), jnp.float32),
        ],
        density,
        tf_bins,
        table,
        order,
    )
    words = call(
        functools.partial(shade_kernel, bricks),
        shape((bricks, 2, owned // LANES, LANES), jnp.int32),
        plane_far,
        plane_near,
        row_near,
        row_far,
        density,
        first,
        second,
        depth,
    )
    words = lax.all_to_all(words, "depth", 0, 0, tiled=True)
    return call(
        functools.partial(merge_kernel, planes, max(owned // across, 1)),
        shape((4, owned), jnp.float32),
        before,
        words,
    )


def solution(mesh):
    in_specs = (P("depth", "strip", None), P("depth", "strip", None), P(), P("strip", None))
    out_specs = P(None, ("strip", "depth"))
    return jax.shard_map(
        per_device, mesh=mesh, in_specs=in_specs, out_specs=out_specs, check_vma=False
    )
```

```python
import functools

import jax
import jax.numpy as jnp
from jax import lax
from jax.experimental import pallas as pl
from jax.experimental.pallas import tpu as pltpu
from jax.sharding import PartitionSpec as P

LIGHT = (0.36, 0.48, 0.8)
SHADE_GAIN = 1.5
LOG2E = 1.4426950408889634
LANES = 128
VMEM_BYTES = 8 * 1024 * 1024

MAX_DENSITY = 6.0
MAX_LOOKED = 2.0

COLOUR_STEPS = 2048.0
COLOUR_LOW = -28.0
CODE_MAX = 65535.0


def depth_scale(planes, total_planes):
    return MAX_LOOKED * (1.0 + MAX_DENSITY * MAX_DENSITY) * LOG2E * planes / total_planes


def pairs(count, start):
    swaps = []
    for i in range(start, count - 1, 2):
        swaps += [(i, i + 1), (i + 1, i)]
    return swaps


def partner_exists(index, count, start):
    lower = index % 2 == start
    return jnp.where(lower, index + 1 < count, index > 0)


def edges_kernel(
    density_hbm,
    bins_hbm,
    table_hbm,
    order_hbm,
    density_ref,
    bins_ref,
    table_ref,
    order_ref,
    plane_near,
    plane_far,
    row_near,
    row_far,
    small_ref,
    semaphores,
):
    density_copy = pltpu.make_async_copy(density_hbm, density_ref, semaphores.at[0])
    bins_copy = pltpu.make_async_copy(bins_hbm, bins_ref, semaphores.at[1])
    density_copy.start()
    bins_copy.start()
    table_copy = pltpu.make_async_copy(table_hbm, small_ref, semaphores.at[2])
    order_copy = pltpu.make_async_copy(order_hbm, order_ref, semaphores.at[3])
    table_copy.start()
    order_copy.start()
    table_ref[...] = jnp.zeros_like(table_ref)
    planes, height, _ = density_ref.shape
    odd_brick = lax.axis_index("depth") % 2
    odd_strip = lax.axis_index("strip") % 2 == 1
    density_copy.wait()
    plane_near[...] = density_ref[pl.ds((1 - odd_brick) * (planes - 1), 1)]
    plane_far[...] = density_ref[pl.ds(odd_brick * (planes - 1), 1)]
    head, tail = density_ref[:, 0, :], density_ref[:, height - 1, :]
    row_near[:, 0, :] = tail
    row_far[:, 0, :] = head
    table_copy.wait()
    table_ref[:, : small_ref.shape[1]] = small_ref[...]
    order_copy.wait()
    bins_copy.wait()


def swap(cells, axis, start):
    bricks, strips = lax.axis_size("depth"), lax.axis_size("strip")
    count = bricks if axis == "depth" else strips
    swaps = pairs(count, start)
    spare = [i for i in range(count) if (i, i + 1) not in swaps and (i, i - 1) not in swaps]
    if axis == "depth":
        links = [((a, s), (b, s)) for a, b in swaps for s in range(strips)]
        if strips % 2 == 0:
            links += [((a, s), (a, s ^ 1)) for a in spare for s in range(strips)]
    else:
        if len(spare) == 2:
            swaps = swaps + [tuple(spare), tuple(spare[::-1])]
        links = [((d, a), (d, b)) for a, b in swaps for d in range(bricks)]
    flat = [(a * strips + s, b * strips + t) for (a, s), (b, t) in links]
    return lax.ppermute(cells, ("depth", "strip"), flat)


def masked(cells, axis, start):
    exists = partner_exists(lax.axis_index(axis), lax.axis_size(axis), start)
    return jnp.where(exists, cells, 0.0)


def tiles_of(value):
    return [value[:, t : t + LANES] for t in range(0, value.shape[1], LANES)]


def lane_next(tiles, lane):
    rolled = [pltpu.roll(v, LANES - 1, 1) for v in tiles] + [0.0]
    return [jnp.where(lane < LANES - 1, rolled[t], rolled[t + 1]) for t in range(len(tiles))]


def lane_previous(tiles, lane):
    rolled = [0.0] + [pltpu.roll(v, 1, 1) for v in tiles]
    return [jnp.where(lane > 0, rolled[t + 1], rolled[t]) for t in range(len(tiles))]


def lane_shift(tiles, lane, shift, beyond):
    amount = (LANES - shift) % LANES
    rolled = [pltpu.roll(v, amount, 1) for v in tiles] + [beyond]
    return [jnp.where(lane < LANES - shift, rolled[t], rolled[t + 1]) for t in range(len(tiles))]


def light_kernel(
    bricks,
    density_ref,
    bins_ref,
    table_ref,
    order_ref,
    first_ref,
    second_ref,
    depth_ref,
    before_ref,
):
    planes, height, across = density_ref.shape
    total_planes = planes * bricks
    count = across // LANES
    f32 = jnp.float32
    lane = lax.broadcasted_iota(jnp.int32, (height, LANES), 1)
    table = [jnp.broadcast_to(table_ref[c : c + 1, :], (height, LANES)) for c in range(4)]
    table[0] = table[0] * (LOG2E / total_planes)
    depth = [jnp.zeros((height, LANES), f32)] * count
    for p in range(planes):
        plane_index = lax.axis_index("depth") * planes + p
        shift = (3 * plane_index) // 8
        fraction = ((3 * plane_index) % 8).astype(f32) / 8.0
        cells = lane_shift(tiles_of(density_ref[p].astype(f32)), lane, shift, 0.0)
        bins = lane_shift(tiles_of(bins_ref[p]), lane, shift, LANES - 1)
        fields = [[], [], [], []]
        for t in range(count):
            looked = [
                jnp.take_along_axis(entry, bins[t], axis=1, mode="promise_in_bounds")
                for entry in table
            ]
            extinction = looked[0] * (1.0 + cells[t] * cells[t])
            opacity = 1.0 - jnp.exp2(-extinction)
            fields[0].append(extinction)
            for c in range(3):
                fields[c + 1].append(looked[c + 1] * opacity)
        after = [lane_next(field, lane) for field in fields]
        for t in range(count):
            cols = slice(t * LANES, (t + 1) * LANES)
            through = jnp.exp2(-depth[t])
            through_second = through * fraction
            through_first = through - through_second
            for c in range(3):
                first_ref[p, c, :, cols] = through_first * fields[c + 1][t]
                second_ref[p, c, :, cols] = through_second * after[c + 1][t]
            depth[t] = depth[t] + (
                fields[0][t] + fraction * (after[0][t] - fields[0][t])
            )
    depth_factor = CODE_MAX / depth_scale(planes, total_planes)
    for t in range(count):
        code = jnp.minimum(depth[t] * depth_factor, CODE_MAX)
        depth_ref[:, t * LANES : (t + 1) * LANES] = (code + 0.5).astype(jnp.int32)
    slot = lax.broadcasted_iota(jnp.int32, (bricks, LANES), 0)
    place = jnp.zeros((bricks, LANES), jnp.int32)
    for k in range(bricks):
        brick = jnp.broadcast_to(order_ref[0:1, k : k + 1], (bricks, LANES))
        place = jnp.where(slot == brick, k, place)
    for b in range(bricks):
        before_ref[b] = (place < place[b : b + 1, :]).astype(f32)


def shade_kernel(
    bricks,
    plane_far,
    plane_near,
    row_far,
    row_near,
    density_ref,
    first_ref,
    second_ref,
    depth_ref,
    out_ref,
):
    planes, height, across = density_ref.shape
    count = across // LANES
    f32 = jnp.float32
    odd_brick = lax.axis_index("depth") % 2 == 1
    odd_strip = lax.axis_index("strip") % 2 == 1
    lane = lax.broadcasted_iota(jnp.int32, (height, LANES), 1)
    row = lax.broadcasted_iota(jnp.int32, (height, LANES), 0)
    near = masked(plane_near[0].astype(f32), "depth", 0)
    far = masked(plane_far[0].astype(f32), "depth", 1)
    beneath = tiles_of(jnp.where(odd_brick, near, far))
    overhead = tiles_of(jnp.where(odd_brick, far, near))
    strip = lax.axis_index("strip")
    above = jnp.where(strip > 0, row_near[:, 0, :].astype(f32), 0.0)
    below = jnp.where(strip < lax.axis_size("strip") - 1, row_far[:, 0, :].astype(f32), 0.0)
    stack = [beneath]
    stack += [tiles_of(density_ref[p].astype(f32)) for p in range(planes)]
    stack += [overhead]
    gain = SHADE_GAIN * LOG2E
    colour = [[None] * count for _ in range(3)]
    for p in range(planes):
        shift = (3 * (lax.axis_index("depth") * planes + p)) // 8
        centre = stack[p + 1]
        ahead, behind = lane_next(centre, lane), lane_previous(centre, lane)
        shade = []
        for t in range(count):
            cols = slice(t * LANES, (t + 1) * LANES)
            v = centre[t]
            up = jnp.where(row == 0, above[p : p + 1, cols], pltpu.roll(v, 1, 0))
            down = jnp.where(
                row == height - 1, below[p : p + 1, cols], pltpu.roll(v, height - 1, 0)
            )
            dx = ahead[t] - behind[t]
            dy = down - up
            dz = stack[p + 2][t] - stack[p][t]
            lit = (LIGHT[0] * gain) * dx + (LIGHT[1] * gain) * dy + (LIGHT[2] * gain) * dz
            shade.append(jnp.exp2(lit * lax.rsqrt(4.0 + dx * dx + dy * dy + dz * dz)))
        shade = lane_shift(shade, lane, shift, 0.0)
        after = lane_next(shade, lane)
        for t in range(count):
            cols = slice(t * LANES, (t + 1) * LANES)
            for c in range(3):
                term = first_ref[p, c, :, cols] * shade[t] + second_ref[p, c, :, cols] * after[t]
                colour[c][t] = term if p == 0 else colour[c][t] + term

    words = [[], []]
    for t in range(count):
        codes = [depth_ref[:, t * LANES : (t + 1) * LANES]]
        for c in range(3):
            code = jnp.log2(colour[c][t]) * COLOUR_STEPS + (0.5 - COLOUR_LOW * COLOUR_STEPS)
            codes.append(jnp.minimum(jnp.maximum(code, 0.0), CODE_MAX).astype(jnp.int32))
        words[0].append(codes[0] | (codes[1] << 16))
        words[1].append(codes[2] | (codes[3] << 16))
    owned = height * across // bricks
    tall, wide = max(owned // across, 1), min(owned, across)
    for owner in range(bricks):
        top, left = owner * owned // across, owner * owned % across
        for w in range(2):
            for t in range(wide // LANES):
                out_ref[owner, w, t * tall : (t + 1) * tall, :] = words[w][left // LANES + t][
                    top : top + tall, :
                ]


def merge_kernel(planes, tall, before_ref, words_ref, out_ref):
    bricks, _, rows, _ = words_ref.shape
    f32 = jnp.float32
    depth_unit = depth_scale(planes, planes * bricks) / CODE_MAX
    depth, codes = [], []
    for b in range(bricks):
        low, high = words_ref[b, 0], words_ref[b, 1]
        depth.append((low & 0xFFFF).astype(f32) * depth_unit)
        codes.append(
            [lax.shift_right_logical(low, 16), high & 0xFFFF, lax.shift_right_logical(high, 16)]
        )
    colour = [jnp.zeros((rows, LANES), f32)] * 3
    for b in range(bricks):
        base = jnp.full((rows, LANES), COLOUR_LOW, f32)
        for other in range(bricks):
            if other != b:
                base = base - before_ref[b, other : other + 1, :] * depth[other]
        for c in range(3):
            term = jnp.exp2(codes[b][c].astype(f32) * (1.0 / COLOUR_STEPS) + base)
            colour[c] = colour[c] + jnp.where(codes[b][c] > 0, term, 0.0)
    image = colour + [jnp.exp2(-sum(depth))]
    wide = rows // tall
    for c in range(4):
        for r in range(tall):
            for t in range(wide):
                at = (r * wide + t) * LANES
                out_ref[c : c + 1, at : at + LANES] = image[c][t * tall + r : t * tall + r + 1, :]


def call(kernel, out_shape, *operands, spaces=None, scratch=()):
    vmem = pl.BlockSpec(memory_space=pltpu.VMEM)
    spaces = spaces or {}
    return pl.pallas_call(
        kernel,
        out_shape=out_shape,
        in_specs=[
            pl.BlockSpec(memory_space=spaces.get(i, pltpu.VMEM)) for i in range(len(operands))
        ],
        out_specs=jax.tree.map(lambda _: vmem, out_shape),
        scratch_shapes=scratch,
        compiler_params=pltpu.CompilerParams(vmem_limit_bytes=VMEM_BYTES),
    )(*operands)


def per_device(density, tf_bins, tf_table, brick_order):
    planes, height, across = density.shape
    bricks = lax.axis_size("depth")
    owned = height * across // bricks
    shape = jax.ShapeDtypeStruct
    plane = shape((1, height, across), density.dtype)
    rows = shape((planes, 1, across), density.dtype)
    density, tf_bins, table, order, plane_near, plane_far, row_near, row_far = call(
        edges_kernel,
        [
            shape(density.shape, density.dtype),
            shape(tf_bins.shape, tf_bins.dtype),
            shape((tf_table.shape[0], LANES), tf_table.dtype),
            shape(brick_order.shape, brick_order.dtype),
            plane,
            plane,
            rows,
            rows,
        ],
        *[
            pltpu.with_memory_space_constraint(argument, pltpu.HBM)
            for argument in (density, tf_bins, tf_table, brick_order)
        ],
        spaces={i: pltpu.HBM for i in range(4)},
        scratch=[pltpu.VMEM(tf_table.shape, tf_table.dtype), pltpu.SemaphoreType.DMA((4,))],
    )
    plane_far = swap(plane_far, "depth", 1)
    plane_near = swap(plane_near, "depth", 0)
    count = lax.axis_size("strip")
    row_near = lax.ppermute(row_near, "strip", [(i, (i + 1) % count) for i in range(count)])
    row_far = lax.ppermute(row_far, "strip", [(i, (i - 1) % count) for i in range(count)])
    sheared = shape((planes, 3, height, across), jnp.float32)
    first, second, depth, before = call(
        functools.partial(light_kernel, bricks),
        [
            sheared,
            sheared,
            shape((height, across), jnp.int32),
            shape((bricks, bricks, LANES), jnp.float32),
        ],
        density,
        tf_bins,
        table,
        order,
    )
    words = call(
        functools.partial(shade_kernel, bricks),
        shape((bricks, 2, owned // LANES, LANES), jnp.int32),
        plane_far,
        plane_near,
        row_far,
        row_near,
        density,
        first,
        second,
        depth,
    )
    words = lax.all_to_all(words, "depth", 0, 0, tiled=True)
    return call(
        functools.partial(merge_kernel, planes, max(owned // across, 1)),
        shape((4, owned), jnp.float32),
        before,
        words,
    )


def solution(mesh):
    in_specs = (P("depth", "strip", None), P("depth", "strip", None), P(), P("strip", None))
    out_specs = P(None, ("strip", "depth"))
    return jax.shard_map(
        per_device, mesh=mesh, in_specs=in_specs, out_specs=out_specs, check_vma=False
    )
```

```python
import functools

import jax
import jax.numpy as jnp
from jax import lax
from jax.experimental import pallas as pl
from jax.experimental.pallas import tpu as pltpu
from jax.sharding import PartitionSpec as P

LIGHT = (0.36, 0.48, 0.8)
SHADE_GAIN = 1.5
LOG2E = 1.4426950408889634
LANES = 128
VMEM_BYTES = 8 * 1024 * 1024

MAX_DENSITY = 6.0
MAX_LOOKED = 2.0

COLOUR_STEPS = 2048.0
COLOUR_LOW = -28.0
CODE_MAX = 65535.0


def depth_scale(planes, total_planes):
    return MAX_LOOKED * (1.0 + MAX_DENSITY * MAX_DENSITY) * LOG2E * planes / total_planes


def pairs(count, start):
    swaps = []
    for i in range(start, count - 1, 2):
        swaps += [(i, i + 1), (i + 1, i)]
    return swaps


def partner_exists(index, count, start):
    lower = index % 2 == start
    return jnp.where(lower, index + 1 < count, index > 0)


def edges_kernel(
    density_hbm,
    bins_hbm,
    table_hbm,
    order_hbm,
    density_ref,
    bins_ref,
    table_ref,
    order_ref,
    plane_near,
    plane_far,
    row_tail,
    row_head,
    small_ref,
    semaphores,
):
    density_copy = pltpu.make_async_copy(density_hbm, density_ref, semaphores.at[0])
    bins_copy = pltpu.make_async_copy(bins_hbm, bins_ref, semaphores.at[1])
    density_copy.start()
    bins_copy.start()
    table_copy = pltpu.make_async_copy(table_hbm, small_ref, semaphores.at[2])
    order_copy = pltpu.make_async_copy(order_hbm, order_ref, semaphores.at[3])
    table_copy.start()
    order_copy.start()
    table_ref[...] = jnp.zeros_like(table_ref)
    planes, height, _ = density_ref.shape
    odd_brick = lax.axis_index("depth") % 2
    density_copy.wait()
    plane_near[...] = density_ref[pl.ds((1 - odd_brick) * (planes - 1), 1)]
    plane_far[...] = density_ref[pl.ds(odd_brick * (planes - 1), 1)]
    head, tail = density_ref[:, 0, :], density_ref[:, height - 1, :]
    row_tail[:, 0, :] = tail
    row_head[:, 0, :] = head
    table_copy.wait()
    table_ref[:, : small_ref.shape[1]] = small_ref[...]
    order_copy.wait()
    bins_copy.wait()


def swap_planes(cells, start):
    bricks, strips = lax.axis_size("depth"), lax.axis_size("strip")
    swaps = pairs(bricks, start)
    links = [((a, s), (b, s)) for a, b in swaps for s in range(strips)]
    if strips % 2 == 0:
        spare = [i for i in range(bricks) if i not in dict(swaps)]
        links += [((a, s), (a, s ^ 1)) for a in spare for s in range(strips)]
    flat = [(a * strips + s, b * strips + t) for (a, s), (b, t) in links]
    return lax.ppermute(cells, ("depth", "strip"), flat)


def rotate_rows(cells, step):
    strips = lax.axis_size("strip")
    return lax.ppermute(cells, "strip", [(i, (i + step) % strips) for i in range(strips)])


def masked(cells, axis, start):
    exists = partner_exists(lax.axis_index(axis), lax.axis_size(axis), start)
    return jnp.where(exists, cells, 0.0)


def tiles_of(value):
    return [value[:, t : t + LANES] for t in range(0, value.shape[1], LANES)]


def lane_next(tiles, lane):
    rolled = [pltpu.roll(v, LANES - 1, 1) for v in tiles] + [0.0]
    return [jnp.where(lane < LANES - 1, rolled[t], rolled[t + 1]) for t in range(len(tiles))]


def lane_previous(tiles, lane):
    rolled = [0.0] + [pltpu.roll(v, 1, 1) for v in tiles]
    return [jnp.where(lane > 0, rolled[t + 1], rolled[t]) for t in range(len(tiles))]


def lane_shift(tiles, lane, shift, beyond):
    amount = (LANES - shift) % LANES
    rolled = [pltpu.roll(v, amount, 1) for v in tiles] + [beyond]
    return [jnp.where(lane < LANES - shift, rolled[t], rolled[t + 1]) for t in range(len(tiles))]


def light_kernel(
    bricks,
    density_ref,
    bins_ref,
    table_ref,
    order_ref,
    first_ref,
    second_ref,
    depth_ref,
    before_ref,
):
    planes, height, across = density_ref.shape
    total_planes = planes * bricks
    count = across // LANES
    f32 = jnp.float32
    lane = lax.broadcasted_iota(jnp.int32, (height, LANES), 1)
    table = [jnp.broadcast_to(table_ref[c : c + 1, :], (height, LANES)) for c in range(4)]
    table[0] = table[0] * (LOG2E / total_planes)
    depth = [jnp.zeros((height, LANES), f32)] * count
    for p in range(planes):
        plane_index = lax.axis_index("depth") * planes + p
        shift = (3 * plane_index) // 8
        fraction = ((3 * plane_index) % 8).astype(f32) / 8.0
        cells = lane_shift(tiles_of(density_ref[p].astype(f32)), lane, shift, 0.0)
        bins = lane_shift(tiles_of(bins_ref[p]), lane, shift, LANES - 1)
        fields = [[], [], [], []]
        for t in range(count):
            looked = [
                jnp.take_along_axis(entry, bins[t], axis=1, mode="promise_in_bounds")
                for entry in table
            ]
            extinction = looked[0] * (1.0 + cells[t] * cells[t])
            opacity = 1.0 - jnp.exp2(-extinction)
            fields[0].append(extinction)
            for c in range(3):
                fields[c + 1].append(looked[c + 1] * opacity)
        after = [lane_next(field, lane) for field in fields]
        for t in range(count):
            cols = slice(t * LANES, (t + 1) * LANES)
            through = jnp.exp2(-depth[t])
            through_second = through * fraction
            through_first = through - through_second
            for c in range(3):
                first_ref[p, c, :, cols] = through_first * fields[c + 1][t]
                second_ref[p, c, :, cols] = through_second * after[c + 1][t]
            depth[t] = depth[t] + (
                fields[0][t] + fraction * (after[0][t] - fields[0][t])
            )
    depth_factor = CODE_MAX / depth_scale(planes, total_planes)
    for t in range(count):
        code = jnp.minimum(depth[t] * depth_factor, CODE_MAX)
        depth_ref[:, t * LANES : (t + 1) * LANES] = (code + 0.5).astype(jnp.int32)
    slot = lax.broadcasted_iota(jnp.int32, (bricks, LANES), 0)
    place = jnp.zeros((bricks, LANES), jnp.int32)
    for k in range(bricks):
        brick = jnp.broadcast_to(order_ref[0:1, k : k + 1], (bricks, LANES))
        place = jnp.where(slot == brick, k, place)
    for b in range(bricks):
        before_ref[b] = (place < place[b : b + 1, :]).astype(f32)


def shade(
    bricks,
    above,
    plane_far,
    plane_near,
    row_below,
    density_ref,
    first_ref,
    second_ref,
    depth_ref,
    out_ref,
):
    planes, height, across = density_ref.shape
    count = across // LANES
    f32 = jnp.float32
    odd_brick = lax.axis_index("depth") % 2 == 1
    lane = lax.broadcasted_iota(jnp.int32, (height, LANES), 1)
    row = lax.broadcasted_iota(jnp.int32, (height, LANES), 0)
    near = masked(plane_near[0].astype(f32), "depth", 0)
    far = masked(plane_far[0].astype(f32), "depth", 1)
    beneath = tiles_of(jnp.where(odd_brick, near, far))
    overhead = tiles_of(jnp.where(odd_brick, far, near))
    strip = lax.axis_index("strip")
    below = jnp.where(strip < lax.axis_size("strip") - 1, row_below[:, 0, :].astype(f32), 0.0)
    stack = [beneath]
    stack += [tiles_of(density_ref[p].astype(f32)) for p in range(planes)]
    stack += [overhead]
    gain = SHADE_GAIN * LOG2E
    colour = [[None] * count for _ in range(3)]
    for p in range(planes):
        shift = (3 * (lax.axis_index("depth") * planes + p)) // 8
        centre = stack[p + 1]
        ahead, behind = lane_next(centre, lane), lane_previous(centre, lane)
        shade = []
        for t in range(count):
            cols = slice(t * LANES, (t + 1) * LANES)
            v = centre[t]
            up = jnp.where(row == 0, above[p : p + 1, cols], pltpu.roll(v, 1, 0))
            down = jnp.where(
                row == height - 1, below[p : p + 1, cols], pltpu.roll(v, height - 1, 0)
            )
            dx = ahead[t] - behind[t]
            dy = down - up
            dz = stack[p + 2][t] - stack[p][t]
            lit = (LIGHT[0] * gain) * dx + (LIGHT[1] * gain) * dy + (LIGHT[2] * gain) * dz
            shade.append(jnp.exp2(lit * lax.rsqrt(4.0 + dx * dx + dy * dy + dz * dz)))
        shade = lane_shift(shade, lane, shift, 0.0)
        after = lane_next(shade, lane)
        for t in range(count):
            cols = slice(t * LANES, (t + 1) * LANES)
            for c in range(3):
                term = first_ref[p, c, :, cols] * shade[t] + second_ref[p, c, :, cols] * after[t]
                colour[c][t] = term if p == 0 else colour[c][t] + term

    words = [[], []]
    for t in range(count):
        codes = [depth_ref[:, t * LANES : (t + 1) * LANES]]
        for c in range(3):
            code = jnp.log2(colour[c][t]) * COLOUR_STEPS + (0.5 - COLOUR_LOW * COLOUR_STEPS)
            codes.append(jnp.minimum(jnp.maximum(code, 0.0), CODE_MAX).astype(jnp.int32))
        words[0].append(codes[0] | (codes[1] << 16))
        words[1].append(codes[2] | (codes[3] << 16))
    owned = height * across // bricks
    tall, wide = max(owned // across, 1), min(owned, across)
    for owner in range(bricks):
        top, left = owner * owned // across, owner * owned % across
        for w in range(2):
            for t in range(wide // LANES):
                out_ref[owner, w, t * tall : (t + 1) * tall, :] = words[w][left // LANES + t][
                    top : top + tall, :
                ]


def top_strip_kernel(bricks, *refs):
    planes, _, across = refs[3].shape

    @pl.when(lax.axis_index("strip") == 0)
    def _():
        shade(bricks, jnp.zeros((planes, across), jnp.float32), *refs)


def other_strips_kernel(bricks, *refs):
    *refs, row_above, top_words_ref, out_ref = refs

    @pl.when(lax.axis_index("strip") == 0)
    def _():
        out_ref[...] = top_words_ref[...]

    @pl.when(lax.axis_index("strip") > 0)
    def _():
        shade(bricks, row_above[:, 0, :].astype(jnp.float32), *refs, out_ref)


def merge_kernel(planes, tall, before_ref, words_ref, out_ref):
    bricks, _, rows, _ = words_ref.shape
    f32 = jnp.float32
    depth_unit = depth_scale(planes, planes * bricks) / CODE_MAX
    depth, codes = [], []
    for b in range(bricks):
        low, high = words_ref[b, 0], words_ref[b, 1]
        depth.append((low & 0xFFFF).astype(f32) * depth_unit)
        codes.append(
            [lax.shift_right_logical(low, 16), high & 0xFFFF, lax.shift_right_logical(high, 16)]
        )
    colour = [jnp.zeros((rows, LANES), f32)] * 3
    for b in range(bricks):
        base = jnp.full((rows, LANES), COLOUR_LOW, f32)
        for other in range(bricks):
            if other != b:
                base = base - before_ref[b, other : other + 1, :] * depth[other]
        for c in range(3):
            term = jnp.exp2(codes[b][c].astype(f32) * (1.0 / COLOUR_STEPS) + base)
            colour[c] = colour[c] + jnp.where(codes[b][c] > 0, term, 0.0)
    image = colour + [jnp.exp2(-sum(depth))]
    wide = rows // tall
    for c in range(4):
        for r in range(tall):
            for t in range(wide):
                at = (r * wide + t) * LANES
                out_ref[c : c + 1, at : at + LANES] = image[c][t * tall + r : t * tall + r + 1, :]


def call(kernel, out_shape, *operands, spaces=None, scratch=()):
    vmem = pl.BlockSpec(memory_space=pltpu.VMEM)
    spaces = spaces or {}
    return pl.pallas_call(
        kernel,
        out_shape=out_shape,
        in_specs=[
            pl.BlockSpec(memory_space=spaces.get(i, pltpu.VMEM)) for i in range(len(operands))
        ],
        out_specs=jax.tree.map(lambda _: vmem, out_shape),
        scratch_shapes=scratch,
        compiler_params=pltpu.CompilerParams(vmem_limit_bytes=VMEM_BYTES),
    )(*operands)


def per_device(density, tf_bins, tf_table, brick_order):
    planes, height, across = density.shape
    bricks = lax.axis_size("depth")
    owned = height * across // bricks
    shape = jax.ShapeDtypeStruct
    plane = shape((1, height, across), density.dtype)
    rows = shape((planes, 1, across), density.dtype)
    density, tf_bins, table, order, plane_near, plane_far, row_tail, row_head = call(
        edges_kernel,
        [
            shape(density.shape, density.dtype),
            shape(tf_bins.shape, tf_bins.dtype),
            shape((tf_table.shape[0], LANES), tf_table.dtype),
            shape(brick_order.shape, brick_order.dtype),
            plane,
            plane,
            rows,
            rows,
        ],
        *[
            pltpu.with_memory_space_constraint(argument, pltpu.HBM)
            for argument in (density, tf_bins, tf_table, brick_order)
        ],
        spaces={i: pltpu.HBM for i in range(4)},
        scratch=[pltpu.VMEM(tf_table.shape, tf_table.dtype), pltpu.SemaphoreType.DMA((4,))],
    )
    plane_far = swap_planes(plane_far, 1)
    plane_near = swap_planes(plane_near, 0)
    row_below = rotate_rows(row_head, -1)
    row_above = rotate_rows(row_tail, 1)
    sheared = shape((planes, 3, height, across), jnp.float32)
    first, second, depth, before = call(
        functools.partial(light_kernel, bricks),
        [
            sheared,
            sheared,
            shape((height, across), jnp.int32),
            shape((bricks, bricks, LANES), jnp.float32),
        ],
        density,
        tf_bins,
        table,
        order,
    )
    words_shape = shape((bricks, 2, owned // LANES, LANES), jnp.int32)
    operands = (plane_far, plane_near, row_below, density, first, second, depth)
    words = call(functools.partial(top_strip_kernel, bricks), words_shape, *operands)
    words = call(
        functools.partial(other_strips_kernel, bricks), words_shape, *operands, row_above, words
    )
    words = lax.all_to_all(words, "depth", 0, 0, tiled=True)
    return call(
        functools.partial(merge_kernel, planes, max(owned // across, 1)),
        shape((4, owned), jnp.float32),
        before,
        words,
    )


def solution(mesh):
    in_specs = (P("depth", "strip", None), P("depth", "strip", None), P(), P("strip", None))
    out_specs = P(None, ("strip", "depth"))
    return jax.shard_map(
        per_device, mesh=mesh, in_specs=in_specs, out_specs=out_specs, check_vma=False
    )
```

```python
import functools

import jax
import jax.numpy as jnp
from jax import lax
from jax.experimental import pallas as pl
from jax.experimental.pallas import tpu as pltpu
from jax.sharding import PartitionSpec as P

LIGHT = (0.36, 0.48, 0.8)
SHADE_GAIN = 1.5
LOG2E = 1.4426950408889634
LANES = 128
VMEM_BYTES = 8 * 1024 * 1024

MAX_DENSITY = 6.0
MAX_LOOKED = 2.0

COLOUR_STEPS = 2048.0
COLOUR_LOW = -28.0
CODE_MAX = 65535.0


def depth_scale(planes, total_planes):
    return MAX_LOOKED * (1.0 + MAX_DENSITY * MAX_DENSITY) * LOG2E * planes / total_planes


def pairs(count, start):
    swaps = []
    for i in range(start, count - 1, 2):
        swaps += [(i, i + 1), (i + 1, i)]
    return swaps


def partner_exists(index, count, start):
    lower = index % 2 == start
    return jnp.where(lower, index + 1 < count, index > 0)


def edges_kernel(
    density_hbm,
    bins_hbm,
    table_hbm,
    order_hbm,
    density_ref,
    bins_ref,
    table_ref,
    order_ref,
    plane_near,
    plane_far,
    row_tail,
    row_head,
    small_ref,
    semaphores,
):
    density_copy = pltpu.make_async_copy(density_hbm, density_ref, semaphores.at[0])
    bins_copy = pltpu.make_async_copy(bins_hbm, bins_ref, semaphores.at[1])
    density_copy.start()
    bins_copy.start()
    table_copy = pltpu.make_async_copy(table_hbm, small_ref, semaphores.at[2])
    order_copy = pltpu.make_async_copy(order_hbm, order_ref, semaphores.at[3])
    table_copy.start()
    order_copy.start()
    table_ref[...] = jnp.zeros_like(table_ref)
    planes, height, _ = density_ref.shape
    odd_brick = lax.axis_index("depth") % 2
    density_copy.wait()
    plane_near[...] = density_ref[pl.ds((1 - odd_brick) * (planes - 1), 1)]
    plane_far[...] = density_ref[pl.ds(odd_brick * (planes - 1), 1)]
    for p in range(planes):
        rows = density_ref[p].astype(jnp.float32)
        row_tail[p] = rows[height - 1 : height, :].astype(row_tail.dtype)
        row_head[p] = rows[0:1, :].astype(row_head.dtype)
    table_copy.wait()
    table_ref[:, : small_ref.shape[1]] = small_ref[...]
    order_copy.wait()
    bins_copy.wait()


def swap_planes(cells, start):
    bricks, strips = lax.axis_size("depth"), lax.axis_size("strip")
    swaps = pairs(bricks, start)
    links = [((a, s), (b, s)) for a, b in swaps for s in range(strips)]
    if strips % 2 == 0:
        spare = [i for i in range(bricks) if i not in dict(swaps)]
        links += [((a, s), (a, s ^ 1)) for a in spare for s in range(strips)]
    flat = [(a * strips + s, b * strips + t) for (a, s), (b, t) in links]
    return lax.ppermute(cells, ("depth", "strip"), flat)


def rotate_rows(cells, step):
    strips = lax.axis_size("strip")
    return lax.ppermute(cells, "strip", [(i, (i + step) % strips) for i in range(strips)])


def masked(cells, axis, start):
    exists = partner_exists(lax.axis_index(axis), lax.axis_size(axis), start)
    return jnp.where(exists, cells, 0.0)


def tiles_of(value):
    return [value[:, t : t + LANES] for t in range(0, value.shape[1], LANES)]


def lane_next(tiles, lane):
    rolled = [pltpu.roll(v, LANES - 1, 1) for v in tiles] + [0.0]
    return [jnp.where(lane < LANES - 1, rolled[t], rolled[t + 1]) for t in range(len(tiles))]


def lane_previous(tiles, lane):
    rolled = [0.0] + [pltpu.roll(v, 1, 1) for v in tiles]
    return [jnp.where(lane > 0, rolled[t + 1], rolled[t]) for t in range(len(tiles))]


def lane_shift(tiles, lane, shift, beyond):
    amount = (LANES - shift) % LANES
    rolled = [pltpu.roll(v, amount, 1) for v in tiles] + [beyond]
    return [jnp.where(lane < LANES - shift, rolled[t], rolled[t + 1]) for t in range(len(tiles))]


def light_kernel(
    bricks,
    density_ref,
    bins_ref,
    table_ref,
    order_ref,
    first_ref,
    second_ref,
    depth_ref,
    before_ref,
):
    planes, height, across = density_ref.shape
    total_planes = planes * bricks
    count = across // LANES
    f32 = jnp.float32
    lane = lax.broadcasted_iota(jnp.int32, (height, LANES), 1)
    table = [jnp.broadcast_to(table_ref[c : c + 1, :], (height, LANES)) for c in range(4)]
    table[0] = table[0] * (LOG2E / total_planes)
    depth = [jnp.zeros((height, LANES), f32)] * count
    for p in range(planes):
        plane_index = lax.axis_index("depth") * planes + p
        shift = (3 * plane_index) // 8
        fraction = ((3 * plane_index) % 8).astype(f32) / 8.0
        cells = lane_shift(tiles_of(density_ref[p].astype(f32)), lane, shift, 0.0)
        bins = lane_shift(tiles_of(bins_ref[p]), lane, shift, LANES - 1)
        fields = [[], [], [], []]
        for t in range(count):
            looked = [
                jnp.take_along_axis(entry, bins[t], axis=1, mode="promise_in_bounds")
                for entry in table
            ]
            extinction = looked[0] * (1.0 + cells[t] * cells[t])
            opacity = 1.0 - jnp.exp2(-extinction)
            fields[0].append(extinction)
            for c in range(3):
                fields[c + 1].append(looked[c + 1] * opacity)
        after = [lane_next(field, lane) for field in fields]
        for t in range(count):
            cols = slice(t * LANES, (t + 1) * LANES)
            through = jnp.exp2(-depth[t])
            through_second = through * fraction
            through_first = through - through_second
            for c in range(3):
                first_ref[p, c, :, cols] = through_first * fields[c + 1][t]
                second_ref[p, c, :, cols] = through_second * after[c + 1][t]
            depth[t] = depth[t] + (
                fields[0][t] + fraction * (after[0][t] - fields[0][t])
            )
    depth_factor = CODE_MAX / depth_scale(planes, total_planes)
    for t in range(count):
        code = jnp.minimum(depth[t] * depth_factor, CODE_MAX)
        depth_ref[:, t * LANES : (t + 1) * LANES] = (code + 0.5).astype(jnp.int32)
    slot = lax.broadcasted_iota(jnp.int32, (bricks, LANES), 0)
    place = jnp.zeros((bricks, LANES), jnp.int32)
    for k in range(bricks):
        brick = jnp.broadcast_to(order_ref[0:1, k : k + 1], (bricks, LANES))
        place = jnp.where(slot == brick, k, place)
    for b in range(bricks):
        before_ref[b] = (place < place[b : b + 1, :]).astype(f32)


def shade(
    bricks,
    above,
    plane_far,
    plane_near,
    row_below,
    density_ref,
    first_ref,
    second_ref,
    depth_ref,
    out_ref,
):
    planes, height, across = density_ref.shape
    count = across // LANES
    f32 = jnp.float32
    odd_brick = lax.axis_index("depth") % 2 == 1
    lane = lax.broadcasted_iota(jnp.int32, (height, LANES), 1)
    row = lax.broadcasted_iota(jnp.int32, (height, LANES), 0)
    near = masked(plane_near[0].astype(f32), "depth", 0)
    far = masked(plane_far[0].astype(f32), "depth", 1)
    beneath = tiles_of(jnp.where(odd_brick, near, far))
    overhead = tiles_of(jnp.where(odd_brick, far, near))
    strip = lax.axis_index("strip")
    below = jnp.where(strip < lax.axis_size("strip") - 1, row_below[:, 0, :].astype(f32), 0.0)
    stack = [beneath]
    stack += [tiles_of(density_ref[p].astype(f32)) for p in range(planes)]
    stack += [overhead]
    gain = SHADE_GAIN * LOG2E
    colour = [[None] * count for _ in range(3)]
    for p in range(planes):
        shift = (3 * (lax.axis_index("depth") * planes + p)) // 8
        centre = stack[p + 1]
        ahead, behind = lane_next(centre, lane), lane_previous(centre, lane)
        shade = []
        for t in range(count):
            cols = slice(t * LANES, (t + 1) * LANES)
            v = centre[t]
            up = jnp.where(row == 0, above[p : p + 1, cols], pltpu.roll(v, 1, 0))
            down = jnp.where(
                row == height - 1, below[p : p + 1, cols], pltpu.roll(v, height - 1, 0)
            )
            dx = ahead[t] - behind[t]
            dy = down - up
            dz = stack[p + 2][t] - stack[p][t]
            lit = (LIGHT[0] * gain) * dx + (LIGHT[1] * gain) * dy + (LIGHT[2] * gain) * dz
            shade.append(jnp.exp2(lit * lax.rsqrt(4.0 + dx * dx + dy * dy + dz * dz)))
        shade = lane_shift(shade, lane, shift, 0.0)
        after = lane_next(shade, lane)
        for t in range(count):
            cols = slice(t * LANES, (t + 1) * LANES)
            for c in range(3):
                term = first_ref[p, c, :, cols] * shade[t] + second_ref[p, c, :, cols] * after[t]
                colour[c][t] = term if p == 0 else colour[c][t] + term

    words = [[], []]
    for t in range(count):
        codes = [depth_ref[:, t * LANES : (t + 1) * LANES]]
        for c in range(3):
            code = jnp.log2(colour[c][t]) * COLOUR_STEPS + (0.5 - COLOUR_LOW * COLOUR_STEPS)
            codes.append(jnp.minimum(jnp.maximum(code, 0.0), CODE_MAX).astype(jnp.int32))
        words[0].append(codes[0] | (codes[1] << 16))
        words[1].append(codes[2] | (codes[3] << 16))
    owned = height * across // bricks
    tall, wide = max(owned // across, 1), min(owned, across)
    for owner in range(bricks):
        top, left = owner * owned // across, owner * owned % across
        for w in range(2):
            for t in range(wide // LANES):
                out_ref[owner, w, t * tall : (t + 1) * tall, :] = words[w][left // LANES + t][
                    top : top + tall, :
                ]


def top_strip_kernel(bricks, *refs):
    planes, _, across = refs[3].shape

    @pl.when(lax.axis_index("strip") == 0)
    def _():
        shade(bricks, jnp.zeros((planes, across), jnp.float32), *refs)


def other_strips_kernel(bricks, *refs):
    *refs, row_above, top_words_ref, out_ref = refs

    @pl.when(lax.axis_index("strip") == 0)
    def _():
        out_ref[...] = top_words_ref[...]

    @pl.when(lax.axis_index("strip") > 0)
    def _():
        shade(bricks, row_above[:, 0, :].astype(jnp.float32), *refs, out_ref)


def merge_kernel(planes, tall, before_ref, words_ref, out_ref):
    bricks, _, rows, _ = words_ref.shape
    f32 = jnp.float32
    depth_unit = depth_scale(planes, planes * bricks) / CODE_MAX
    depth, codes = [], []
    for b in range(bricks):
        low, high = words_ref[b, 0], words_ref[b, 1]
        depth.append((low & 0xFFFF).astype(f32) * depth_unit)
        codes.append(
            [lax.shift_right_logical(low, 16), high & 0xFFFF, lax.shift_right_logical(high, 16)]
        )
    colour = [jnp.zeros((rows, LANES), f32)] * 3
    for b in range(bricks):
        base = jnp.full((rows, LANES), COLOUR_LOW, f32)
        for other in range(bricks):
            if other != b:
                base = base - before_ref[b, other : other + 1, :] * depth[other]
        for c in range(3):
            term = jnp.exp2(codes[b][c].astype(f32) * (1.0 / COLOUR_STEPS) + base)
            colour[c] = colour[c] + jnp.where(codes[b][c] > 0, term, 0.0)
    image = colour + [jnp.exp2(-sum(depth))]
    wide = rows // tall
    for c in range(4):
        for r in range(tall):
            for t in range(wide):
                at = (r * wide + t) * LANES
                out_ref[c : c + 1, at : at + LANES] = image[c][t * tall + r : t * tall + r + 1, :]


def call(kernel, out_shape, *operands, spaces=None, scratch=()):
    vmem = pl.BlockSpec(memory_space=pltpu.VMEM)
    spaces = spaces or {}
    return pl.pallas_call(
        kernel,
        out_shape=out_shape,
        in_specs=[
            pl.BlockSpec(memory_space=spaces.get(i, pltpu.VMEM)) for i in range(len(operands))
        ],
        out_specs=jax.tree.map(lambda _: vmem, out_shape),
        scratch_shapes=scratch,
        compiler_params=pltpu.CompilerParams(vmem_limit_bytes=VMEM_BYTES),
    )(*operands)


def per_device(density, tf_bins, tf_table, brick_order):
    planes, height, across = density.shape
    bricks = lax.axis_size("depth")
    owned = height * across // bricks
    shape = jax.ShapeDtypeStruct
    plane = shape((1, height, across), density.dtype)
    rows = shape((planes, 1, across), density.dtype)
    density, tf_bins, table, order, plane_near, plane_far, row_tail, row_head = call(
        edges_kernel,
        [
            shape(density.shape, density.dtype),
            shape(tf_bins.shape, tf_bins.dtype),
            shape((tf_table.shape[0], LANES), tf_table.dtype),
            shape(brick_order.shape, brick_order.dtype),
            plane,
            plane,
            rows,
            rows,
        ],
        *[
            pltpu.with_memory_space_constraint(argument, pltpu.HBM)
            for argument in (density, tf_bins, tf_table, brick_order)
        ],
        spaces={i: pltpu.HBM for i in range(4)},
        scratch=[pltpu.VMEM(tf_table.shape, tf_table.dtype), pltpu.SemaphoreType.DMA((4,))],
    )
    plane_far = swap_planes(plane_far, 1)
    plane_near = swap_planes(plane_near, 0)
    row_below = rotate_rows(row_head, -1)
    row_above = rotate_rows(row_tail, 1)
    sheared = shape((planes, 3, height, across), jnp.float32)
    first, second, depth, before = call(
        functools.partial(light_kernel, bricks),
        [
            sheared,
            sheared,
            shape((height, across), jnp.int32),
            shape((bricks, bricks, LANES), jnp.float32),
        ],
        density,
        tf_bins,
        table,
        order,
    )
    words_shape = shape((bricks, 2, owned // LANES, LANES), jnp.int32)
    operands = (plane_far, plane_near, row_below, density, first, second, depth)
    words = call(functools.partial(top_strip_kernel, bricks), words_shape, *operands)
    words = call(
        functools.partial(other_strips_kernel, bricks), words_shape, *operands, row_above, words
    )
    words = lax.all_to_all(words, "depth", 0, 0, tiled=True)
    return call(
        functools.partial(merge_kernel, planes, max(owned // across, 1)),
        shape((4, owned), jnp.float32),
        before,
        words,
    )


def solution(mesh):
    in_specs = (P("depth", "strip", None), P("depth", "strip", None), P(), P("strip", None))
    out_specs = P(None, ("strip", "depth"))
    return jax.shard_map(
        per_device, mesh=mesh, in_specs=in_specs, out_specs=out_specs, check_vma=False
    )
```

```python
import functools

import jax
import jax.numpy as jnp
from jax import lax
from jax.experimental import pallas as pl
from jax.experimental.pallas import tpu as pltpu
from jax.sharding import PartitionSpec as P

LIGHT = (0.36, 0.48, 0.8)
SHADE_GAIN = 1.5
LOG2E = 1.4426950408889634
LANES = 128
VMEM_BYTES = 8 * 1024 * 1024

MAX_DENSITY = 6.0
MAX_LOOKED = 2.0

COLOUR_STEPS = 2048.0
COLOUR_LOW = -28.0
CODE_MAX = 65535.0


def depth_scale(planes, total_planes):
    return MAX_LOOKED * (1.0 + MAX_DENSITY * MAX_DENSITY) * LOG2E * planes / total_planes


def pairs(count, start):
    swaps = []
    for i in range(start, count - 1, 2):
        swaps += [(i, i + 1), (i + 1, i)]
    return swaps


def partner_exists(index, count, start):
    lower = index % 2 == start
    return jnp.where(lower, index + 1 < count, index > 0)


def edges_kernel(
    density_hbm,
    bins_hbm,
    table_hbm,
    order_hbm,
    density_ref,
    bins_ref,
    table_ref,
    order_ref,
    plane_near,
    plane_far,
    row_tail,
    row_head,
    small_ref,
    semaphores,
):
    density_copy = pltpu.make_async_copy(density_hbm, density_ref, semaphores.at[0])
    density_copy.start()
    odd_strip = lax.axis_index("strip") % 2 == 1

    @pl.when(odd_strip)
    def _():
        pltpu.make_async_copy(bins_hbm, bins_ref, semaphores.at[1]).start()

    table_copy = pltpu.make_async_copy(table_hbm, small_ref, semaphores.at[2])
    order_copy = pltpu.make_async_copy(order_hbm, order_ref, semaphores.at[3])
    table_copy.start()
    order_copy.start()
    table_ref[...] = jnp.zeros_like(table_ref)
    planes, height, _ = density_ref.shape
    odd_brick = lax.axis_index("depth") % 2
    density_copy.wait()
    plane_near[...] = density_ref[pl.ds((1 - odd_brick) * (planes - 1), 1)]
    plane_far[...] = density_ref[pl.ds(odd_brick * (planes - 1), 1)]
    wide = [density_ref[p].astype(jnp.float32) for p in range(planes)]
    tails = jnp.concatenate([rows[height - 1 : height, :] for rows in wide], axis=0)
    heads = jnp.concatenate([rows[0:1, :] for rows in wide], axis=0)
    row_tail[...] = tails.astype(row_tail.dtype)
    row_head[...] = heads.astype(row_head.dtype)
    table_copy.wait()
    table_ref[:, : small_ref.shape[1]] = small_ref[...]
    order_copy.wait()

    @pl.when(odd_strip)
    def _():
        pltpu.make_async_copy(bins_hbm, bins_ref, semaphores.at[1]).wait()


def swap_planes(cells, start):
    bricks, strips = lax.axis_size("depth"), lax.axis_size("strip")
    swaps = pairs(bricks, start)
    links = [((a, s), (b, s)) for a, b in swaps for s in range(strips)]
    if strips % 2 == 0:
        spare = [i for i in range(bricks) if i not in dict(swaps)]
        links += [((a, s), (a, s ^ 1)) for a in spare for s in range(strips)]
    flat = [(a * strips + s, b * strips + t) for (a, s), (b, t) in links]
    return lax.ppermute(cells, ("depth", "strip"), flat)


def rotate_rows(cells, step):
    strips = lax.axis_size("strip")
    return lax.ppermute(cells, "strip", [(i, (i + step) % strips) for i in range(strips)])


def masked(cells, axis, start):
    exists = partner_exists(lax.axis_index(axis), lax.axis_size(axis), start)
    return jnp.where(exists, cells, 0.0)


def tiles_of(value):
    return [value[:, t : t + LANES] for t in range(0, value.shape[1], LANES)]


def lane_next(tiles, lane):
    rolled = [pltpu.roll(v, LANES - 1, 1) for v in tiles] + [0.0]
    return [jnp.where(lane < LANES - 1, rolled[t], rolled[t + 1]) for t in range(len(tiles))]


def lane_previous(tiles, lane):
    rolled = [0.0] + [pltpu.roll(v, 1, 1) for v in tiles]
    return [jnp.where(lane > 0, rolled[t + 1], rolled[t]) for t in range(len(tiles))]


def lane_shift(tiles, lane, shift, beyond):
    amount = (LANES - shift) % LANES
    rolled = [pltpu.roll(v, amount, 1) for v in tiles] + [beyond]
    return [jnp.where(lane < LANES - shift, rolled[t], rolled[t + 1]) for t in range(len(tiles))]


def light_kernel(bricks, bins_hbm, bins_vmem, *refs):
    *refs, bins_scratch, semaphore = refs
    odd_strip = lax.axis_index("strip") % 2 == 1

    @pl.when(odd_strip)
    def _():
        light(bricks, bins_vmem, *refs)

    @pl.when(jnp.logical_not(odd_strip))
    def _():
        bins_copy = pltpu.make_async_copy(bins_hbm, bins_scratch, semaphore)
        bins_copy.start()
        bins_copy.wait()
        light(bricks, bins_scratch, *refs)


def light(
    bricks,
    bins_ref,
    density_ref,
    table_ref,
    order_ref,
    first_ref,
    second_ref,
    depth_ref,
    before_ref,
):
    planes, height, across = density_ref.shape
    total_planes = planes * bricks
    count = across // LANES
    f32 = jnp.float32
    lane = lax.broadcasted_iota(jnp.int32, (height, LANES), 1)
    codes = (table_ref[...] * (CODE_MAX / MAX_LOOKED) + 0.5).astype(jnp.int32)
    table = [
        jnp.broadcast_to(codes[c : c + 1, :] | (codes[c + 1 : c + 2, :] << 16), (height, LANES))
        for c in (0, 2)
    ]
    colour_unit = MAX_LOOKED / CODE_MAX
    extinction_unit = colour_unit * LOG2E / total_planes
    depth = [jnp.zeros((height, LANES), f32)] * count
    for p in range(planes):
        plane_index = lax.axis_index("depth") * planes + p
        shift = (3 * plane_index) // 8
        fraction = ((3 * plane_index) % 8).astype(f32) / 8.0
        cells = lane_shift(tiles_of(density_ref[p].astype(f32)), lane, shift, 0.0)
        bins = lane_shift(tiles_of(bins_ref[p]), lane, shift, LANES - 1)
        fields = [[], [], [], []]
        for t in range(count):
            looked = []
            for entry in table:
                word = jnp.take_along_axis(entry, bins[t], axis=1, mode="promise_in_bounds")
                looked += [(word & 0xFFFF).astype(f32), lax.shift_right_logical(word, 16).astype(f32)]
            extinction = looked[0] * (extinction_unit + extinction_unit * (cells[t] * cells[t]))
            opacity = colour_unit - colour_unit * jnp.exp2(-extinction)
            fields[0].append(extinction)
            for c in range(3):
                fields[c + 1].append(looked[c + 1] * opacity)
        after = [lane_next(field, lane) for field in fields]
        for t in range(count):
            cols = slice(t * LANES, (t + 1) * LANES)
            through = jnp.exp2(-depth[t])
            through_second = through * fraction
            through_first = through - through_second
            for c in range(3):
                first_ref[p, c, :, cols] = through_first * fields[c + 1][t]
                second_ref[p, c, :, cols] = through_second * after[c + 1][t]
            depth[t] = depth[t] + (
                fields[0][t] + fraction * (after[0][t] - fields[0][t])
            )
    depth_factor = CODE_MAX / depth_scale(planes, total_planes)
    for t in range(count):
        code = jnp.minimum(depth[t] * depth_factor, CODE_MAX)
        depth_ref[:, t * LANES : (t + 1) * LANES] = (code + 0.5).astype(jnp.int32)
    slot = lax.broadcasted_iota(jnp.int32, (bricks, LANES), 0)
    place = jnp.zeros((bricks, LANES), jnp.int32)
    for k in range(bricks):
        brick = jnp.broadcast_to(order_ref[0:1, k : k + 1], (bricks, LANES))
        place = jnp.where(slot == brick, k, place)
    for b in range(bricks):
        before_ref[b] = (place < place[b : b + 1, :]).astype(f32)


def shade(
    bricks,
    above,
    plane_far,
    plane_near,
    row_below,
    density_ref,
    first_ref,
    second_ref,
    depth_ref,
    out_ref,
):
    planes, height, across = density_ref.shape
    count = across // LANES
    f32 = jnp.float32
    odd_brick = lax.axis_index("depth") % 2 == 1
    lane = lax.broadcasted_iota(jnp.int32, (height, LANES), 1)
    row = lax.broadcasted_iota(jnp.int32, (height, LANES), 0)
    near = masked(plane_near[0].astype(f32), "depth", 0)
    far = masked(plane_far[0].astype(f32), "depth", 1)
    beneath = tiles_of(jnp.where(odd_brick, near, far))
    overhead = tiles_of(jnp.where(odd_brick, far, near))
    strip = lax.axis_index("strip")
    below = jnp.where(strip < lax.axis_size("strip") - 1, row_below[...].astype(f32), 0.0)
    stack = [beneath]
    stack += [tiles_of(density_ref[p].astype(f32)) for p in range(planes)]
    stack += [overhead]
    gain = SHADE_GAIN * LOG2E
    colour = [[None] * count for _ in range(3)]
    for p in range(planes):
        shift = (3 * (lax.axis_index("depth") * planes + p)) // 8
        centre = stack[p + 1]
        ahead, behind = lane_next(centre, lane), lane_previous(centre, lane)
        shade = []
        for t in range(count):
            cols = slice(t * LANES, (t + 1) * LANES)
            v = centre[t]
            up = jnp.where(row == 0, above[p : p + 1, cols], pltpu.roll(v, 1, 0))
            down = jnp.where(
                row == height - 1, below[p : p + 1, cols], pltpu.roll(v, height - 1, 0)
            )
            dx = ahead[t] - behind[t]
            dy = down - up
            dz = stack[p + 2][t] - stack[p][t]
            lit = (LIGHT[0] * gain) * dx + (LIGHT[1] * gain) * dy + (LIGHT[2] * gain) * dz
            shade.append(jnp.exp2(lit * lax.rsqrt(4.0 + dx * dx + dy * dy + dz * dz)))
        shade = lane_shift(shade, lane, shift, 0.0)
        after = lane_next(shade, lane)
        for t in range(count):
            cols = slice(t * LANES, (t + 1) * LANES)
            for c in range(3):
                term = first_ref[p, c, :, cols] * shade[t] + second_ref[p, c, :, cols] * after[t]
                colour[c][t] = term if p == 0 else colour[c][t] + term

    words = [[], []]
    for t in range(count):
        codes = [depth_ref[:, t * LANES : (t + 1) * LANES]]
        for c in range(3):
            code = jnp.log2(colour[c][t]) * COLOUR_STEPS + (0.5 - COLOUR_LOW * COLOUR_STEPS)
            codes.append(jnp.minimum(jnp.maximum(code, 0.0), CODE_MAX).astype(jnp.int32))
        words[0].append(codes[0] | (codes[1] << 16))
        words[1].append(codes[2] | (codes[3] << 16))
    owned = height * across // bricks
    tall, wide = max(owned // across, 1), min(owned, across)
    for owner in range(bricks):
        top, left = owner * owned // across, owner * owned % across
        for w in range(2):
            for t in range(wide // LANES):
                out_ref[owner, w, t * tall : (t + 1) * tall, :] = words[w][left // LANES + t][
                    top : top + tall, :
                ]


def top_strip_kernel(bricks, *refs):
    planes, _, across = refs[3].shape

    @pl.when(lax.axis_index("strip") == 0)
    def _():
        shade(bricks, jnp.zeros((planes, across), jnp.float32), *refs)


def other_strips_kernel(bricks, *refs):
    *refs, row_above, top_words_ref, out_ref = refs

    @pl.when(lax.axis_index("strip") == 0)
    def _():
        out_ref[...] = top_words_ref[...]

    @pl.when(lax.axis_index("strip") > 0)
    def _():
        shade(bricks, row_above[...].astype(jnp.float32), *refs, out_ref)


def merge_kernel(planes, tall, before_ref, words_ref, out_ref):
    bricks, _, rows, _ = words_ref.shape
    f32 = jnp.float32
    depth_unit = depth_scale(planes, planes * bricks) / CODE_MAX
    depth, codes = [], []
    for b in range(bricks):
        low, high = words_ref[b, 0], words_ref[b, 1]
        depth.append((low & 0xFFFF).astype(f32) * depth_unit)
        codes.append(
            [lax.shift_right_logical(low, 16), high & 0xFFFF, lax.shift_right_logical(high, 16)]
        )
    colour = [jnp.zeros((rows, LANES), f32)] * 3
    for b in range(bricks):
        base = jnp.full((rows, LANES), COLOUR_LOW, f32)
        for other in range(bricks):
            if other != b:
                base = base - before_ref[b, other : other + 1, :] * depth[other]
        for c in range(3):
            term = jnp.exp2(codes[b][c].astype(f32) * (1.0 / COLOUR_STEPS) + base)
            colour[c] = colour[c] + jnp.where(codes[b][c] > 0, term, 0.0)
    image = colour + [jnp.exp2(-sum(depth))]
    wide = rows // tall
    for c in range(4):
        for r in range(tall):
            for t in range(wide):
                at = (r * wide + t) * LANES
                out_ref[c : c + 1, at : at + LANES] = image[c][t * tall + r : t * tall + r + 1, :]


def call(kernel, out_shape, *operands, spaces=None, scratch=()):
    vmem = pl.BlockSpec(memory_space=pltpu.VMEM)
    spaces = spaces or {}
    return pl.pallas_call(
        kernel,
        out_shape=out_shape,
        in_specs=[
            pl.BlockSpec(memory_space=spaces.get(i, pltpu.VMEM)) for i in range(len(operands))
        ],
        out_specs=jax.tree.map(lambda _: vmem, out_shape),
        scratch_shapes=scratch,
        compiler_params=pltpu.CompilerParams(vmem_limit_bytes=VMEM_BYTES),
    )(*operands)


def per_device(density, tf_bins, tf_table, brick_order):
    planes, height, across = density.shape
    bricks = lax.axis_size("depth")
    owned = height * across // bricks
    shape = jax.ShapeDtypeStruct
    plane = shape((1, height, across), density.dtype)
    rows = shape((planes, across), density.dtype)
    arguments = [
        pltpu.with_memory_space_constraint(argument, pltpu.HBM)
        for argument in (density, tf_bins, tf_table, brick_order)
    ]
    density, bins, table, order, plane_near, plane_far, row_tail, row_head = call(
        edges_kernel,
        [
            shape(density.shape, density.dtype),
            shape(tf_bins.shape, tf_bins.dtype),
            shape((tf_table.shape[0], LANES), tf_table.dtype),
            shape(brick_order.shape, brick_order.dtype),
            plane,
            plane,
            rows,
            rows,
        ],
        *arguments,
        spaces={i: pltpu.HBM for i in range(4)},
        scratch=[pltpu.VMEM(tf_table.shape, tf_table.dtype), pltpu.SemaphoreType.DMA((4,))],
    )
    plane_far = swap_planes(plane_far, 1)
    plane_near = swap_planes(plane_near, 0)
    row_below = rotate_rows(row_head, -1)
    row_above = rotate_rows(row_tail, 1)
    sheared = shape((planes, 3, height, across), jnp.float32)
    first, second, depth, before = call(
        functools.partial(light_kernel, bricks),
        [
            sheared,
            sheared,
            shape((height, across), jnp.int32),
            shape((bricks, bricks, LANES), jnp.float32),
        ],
        arguments[1],
        bins,
        density,
        table,
        order,
        spaces={0: pltpu.HBM},
        scratch=[pltpu.VMEM(tf_bins.shape, tf_bins.dtype), pltpu.SemaphoreType.DMA],
    )
    words_shape = shape((bricks, 2, owned // LANES, LANES), jnp.int32)
    operands = (plane_far, plane_near, row_below, density, first, second, depth)
    words = call(functools.partial(top_strip_kernel, bricks), words_shape, *operands)
    words = call(
        functools.partial(other_strips_kernel, bricks), words_shape, *operands, row_above, words
    )
    words = lax.all_to_all(words, "depth", 0, 0, tiled=True)
    return call(
        functools.partial(merge_kernel, planes, max(owned // across, 1)),
        shape((4, owned), jnp.float32),
        before,
        words,
    )


def solution(mesh):
    in_specs = (P("depth", "strip", None), P("depth", "strip", None), P(), P("strip", None))
    out_specs = P(None, ("strip", "depth"))
    return jax.shard_map(
        per_device, mesh=mesh, in_specs=in_specs, out_specs=out_specs, check_vma=False
    )
```

```python
import functools

import jax
import jax.numpy as jnp
from jax import lax
from jax.experimental import pallas as pl
from jax.experimental.pallas import tpu as pltpu
from jax.sharding import PartitionSpec as P

LIGHT = (0.36, 0.48, 0.8)
SHADE_GAIN = 1.5
LOG2E = 1.4426950408889634
LANES = 128
VMEM_BYTES = 8 * 1024 * 1024

MAX_DENSITY = 6.0
MAX_LOOKED = 2.0

COLOUR_STEPS = 2048.0
COLOUR_LOW = -28.0
CODE_MAX = 65535.0


def depth_scale(planes, total_planes):
    return MAX_LOOKED * (1.0 + MAX_DENSITY * MAX_DENSITY) * LOG2E * planes / total_planes


def pairs(count, start):
    swaps = []
    for i in range(start, count - 1, 2):
        swaps += [(i, i + 1), (i + 1, i)]
    return swaps


def partner_exists(index, count, start):
    lower = index % 2 == start
    return jnp.where(lower, index + 1 < count, index > 0)


def edges_kernel(
    density_hbm,
    bins_hbm,
    table_hbm,
    order_hbm,
    density_ref,
    bins_ref,
    table_ref,
    order_ref,
    plane_near,
    plane_far,
    row_tail,
    row_head,
    small_ref,
    semaphores,
):
    density_copy = pltpu.make_async_copy(density_hbm, density_ref, semaphores.at[0])
    density_copy.start()
    odd_strip = lax.axis_index("strip") % 2 == 1

    @pl.when(odd_strip)
    def _():
        pltpu.make_async_copy(bins_hbm, bins_ref, semaphores.at[1]).start()

    table_copy = pltpu.make_async_copy(table_hbm, small_ref, semaphores.at[2])
    order_copy = pltpu.make_async_copy(order_hbm, order_ref, semaphores.at[3])
    table_copy.start()
    order_copy.start()
    table_ref[...] = jnp.zeros_like(table_ref)
    planes, height, _ = density_ref.shape
    odd_brick = lax.axis_index("depth") % 2
    density_copy.wait()
    plane_near[...] = density_ref[pl.ds((1 - odd_brick) * (planes - 1), 1)]
    plane_far[...] = density_ref[pl.ds(odd_brick * (planes - 1), 1)]
    wide = [density_ref[p].astype(jnp.float32) for p in range(planes)]
    tails = jnp.concatenate([rows[height - 1 : height, :] for rows in wide], axis=0)
    heads = jnp.concatenate([rows[0:1, :] for rows in wide], axis=0)
    row_tail[...] = tails.astype(row_tail.dtype)
    row_head[...] = heads.astype(row_head.dtype)
    table_copy.wait()
    table_ref[:, : small_ref.shape[1]] = small_ref[...]
    order_copy.wait()

    @pl.when(odd_strip)
    def _():
        pltpu.make_async_copy(bins_hbm, bins_ref, semaphores.at[1]).wait()


def swap_planes(cells, start):
    bricks, strips = lax.axis_size("depth"), lax.axis_size("strip")
    swaps = pairs(bricks, start)
    links = [((a, s), (b, s)) for a, b in swaps for s in range(strips)]
    if strips % 2 == 0:
        spare = [i for i in range(bricks) if i not in dict(swaps)]
        links += [((a, s), (a, s ^ 1)) for a in spare for s in range(strips)]
    flat = [(a * strips + s, b * strips + t) for (a, s), (b, t) in links]
    return lax.ppermute(cells, ("depth", "strip"), flat)


def rotate_rows(cells, step):
    strips = lax.axis_size("strip")
    return lax.ppermute(cells, "strip", [(i, (i + step) % strips) for i in range(strips)])


def masked(cells, axis, start):
    exists = partner_exists(lax.axis_index(axis), lax.axis_size(axis), start)
    return jnp.where(exists, cells, 0.0)


def tiles_of(value):
    return [value[:, t : t + LANES] for t in range(0, value.shape[1], LANES)]


def lane_next(tiles, lane):
    rolled = [pltpu.roll(v, LANES - 1, 1) for v in tiles] + [0.0]
    return [jnp.where(lane < LANES - 1, rolled[t], rolled[t + 1]) for t in range(len(tiles))]


def lane_previous(tiles, lane):
    rolled = [0.0] + [pltpu.roll(v, 1, 1) for v in tiles]
    return [jnp.where(lane > 0, rolled[t + 1], rolled[t]) for t in range(len(tiles))]


def lane_shift(tiles, lane, shift, beyond):
    amount = (LANES - shift) % LANES
    rolled = [pltpu.roll(v, amount, 1) for v in tiles] + [beyond]
    return [jnp.where(lane < LANES - shift, rolled[t], rolled[t + 1]) for t in range(len(tiles))]


def light_kernel(bricks, bins_hbm, bins_vmem, *refs):
    *refs, bins_scratch, semaphore = refs
    odd_strip = lax.axis_index("strip") % 2 == 1

    @pl.when(odd_strip)
    def _():
        light(bricks, bins_vmem, *refs)

    @pl.when(jnp.logical_not(odd_strip))
    def _():
        bins_copy = pltpu.make_async_copy(bins_hbm, bins_scratch, semaphore)
        bins_copy.start()
        bins_copy.wait()
        light(bricks, bins_scratch, *refs)


def light(
    bricks,
    bins_ref,
    density_ref,
    table_ref,
    order_ref,
    first_ref,
    second_ref,
    depth_ref,
    before_ref,
):
    planes, height, across = density_ref.shape
    total_planes = planes * bricks
    count = across // LANES
    f32 = jnp.float32
    lane = lax.broadcasted_iota(jnp.int32, (height, LANES), 1)
    codes = (table_ref[...] * (CODE_MAX / MAX_LOOKED) + 0.5).astype(jnp.int32)
    table = [
        jnp.broadcast_to(codes[c : c + 1, :] | (codes[c + 1 : c + 2, :] << 16), (height, LANES))
        for c in (0, 2)
    ]
    colour_unit = MAX_LOOKED / CODE_MAX
    extinction_unit = colour_unit * LOG2E / total_planes
    depth = [jnp.zeros((height, LANES), f32)] * count
    for p in range(planes):
        plane_index = lax.axis_index("depth") * planes + p
        shift = (3 * plane_index) // 8
        fraction = ((3 * plane_index) % 8).astype(f32) / 8.0
        cells = lane_shift(tiles_of(density_ref[p].astype(f32)), lane, shift, 0.0)
        bins = lane_shift(tiles_of(bins_ref[p]), lane, shift, LANES - 1)
        fields = [[], [], [], []]
        for t in range(count):
            looked = []
            for entry in table:
                word = jnp.take_along_axis(entry, bins[t], axis=1, mode="promise_in_bounds")
                looked += [(word & 0xFFFF).astype(f32), lax.shift_right_logical(word, 16).astype(f32)]
            extinction = looked[0] * (extinction_unit + extinction_unit * (cells[t] * cells[t]))
            opacity = colour_unit - colour_unit * jnp.exp2(-extinction)
            fields[0].append(extinction)
            for c in range(3):
                fields[c + 1].append(looked[c + 1] * opacity)
        after = [lane_next(field, lane) for field in fields]
        for t in range(count):
            cols = slice(t * LANES, (t + 1) * LANES)
            through = jnp.exp2(-depth[t])
            through_second = through * fraction
            through_first = through - through_second
            for c in range(3):
                first_ref[p, c, :, cols] = through_first * fields[c + 1][t]
                second_ref[p, c, :, cols] = through_second * after[c + 1][t]
            depth[t] = depth[t] + (
                fields[0][t] + fraction * (after[0][t] - fields[0][t])
            )
    depth_factor = CODE_MAX / depth_scale(planes, total_planes)
    for t in range(count):
        code = jnp.minimum(depth[t] * depth_factor, CODE_MAX)
        depth_ref[:, t * LANES : (t + 1) * LANES] = (code + 0.5).astype(jnp.int32)
    slot = lax.broadcasted_iota(jnp.int32, (bricks, LANES), 0)
    place = jnp.zeros((bricks, LANES), jnp.int32)
    for k in range(bricks):
        brick = jnp.broadcast_to(order_ref[0:1, k : k + 1], (bricks, LANES))
        place = jnp.where(slot == brick, k, place)
    for b in range(bricks):
        before_ref[b] = (place < place[b : b + 1, :]).astype(f32)


def shade(
    bricks,
    above,
    plane_far,
    plane_near,
    row_below,
    density_ref,
    first_ref,
    second_ref,
    depth_ref,
    out_ref,
):
    planes, height, across = density_ref.shape
    count = across // LANES
    f32 = jnp.float32
    odd_brick = lax.axis_index("depth") % 2 == 1
    lane = lax.broadcasted_iota(jnp.int32, (height, LANES), 1)
    row = lax.broadcasted_iota(jnp.int32, (height, LANES), 0)
    near = masked(plane_near[0].astype(f32), "depth", 0)
    far = masked(plane_far[0].astype(f32), "depth", 1)
    beneath = tiles_of(jnp.where(odd_brick, near, far))
    overhead = tiles_of(jnp.where(odd_brick, far, near))
    strip = lax.axis_index("strip")
    below = jnp.where(strip < lax.axis_size("strip") - 1, row_below[...].astype(f32), 0.0)
    stack = [beneath]
    stack += [tiles_of(density_ref[p].astype(f32)) for p in range(planes)]
    stack += [overhead]
    gain = SHADE_GAIN * LOG2E
    colour = [[None] * count for _ in range(3)]
    for p in range(planes):
        shift = (3 * (lax.axis_index("depth") * planes + p)) // 8
        centre = stack[p + 1]
        ahead, behind = lane_next(centre, lane), lane_previous(centre, lane)
        shade = []
        for t in range(count):
            cols = slice(t * LANES, (t + 1) * LANES)
            v = centre[t]
            up = jnp.where(row == 0, above[p : p + 1, cols], pltpu.roll(v, 1, 0))
            down = jnp.where(
                row == height - 1, below[p : p + 1, cols], pltpu.roll(v, height - 1, 0)
            )
            dx = ahead[t] - behind[t]
            dy = down - up
            dz = stack[p + 2][t] - stack[p][t]
            lit = (LIGHT[0] * gain) * dx + (LIGHT[1] * gain) * dy + (LIGHT[2] * gain) * dz
            shade.append(jnp.exp2(lit * lax.rsqrt(4.0 + dx * dx + dy * dy + dz * dz)))
        shade = lane_shift(shade, lane, shift, 0.0)
        after = lane_next(shade, lane)
        for t in range(count):
            cols = slice(t * LANES, (t + 1) * LANES)
            for c in range(3):
                term = first_ref[p, c, :, cols] * shade[t] + second_ref[p, c, :, cols] * after[t]
                colour[c][t] = term if p == 0 else colour[c][t] + term

    words = [[], []]
    for t in range(count):
        codes = [depth_ref[:, t * LANES : (t + 1) * LANES]]
        for c in range(3):
            code = jnp.log2(colour[c][t]) * COLOUR_STEPS + (0.5 - COLOUR_LOW * COLOUR_STEPS)
            codes.append(jnp.minimum(jnp.maximum(code, 0.0), CODE_MAX).astype(jnp.int32))
        words[0].append(codes[0] | (codes[1] << 16))
        words[1].append(codes[2] | (codes[3] << 16))
    owned = height * across // bricks
    tall, wide = max(owned // across, 1), min(owned, across)
    for owner in range(bricks):
        top, left = owner * owned // across, owner * owned % across
        for w in range(2):
            for t in range(wide // LANES):
                for r in range(tall):
                    out_ref[owner, w, r * (wide // LANES) + t : r * (wide // LANES) + t + 1, :] = words[
                        w
                    ][left // LANES + t][top + r : top + r + 1, :]


def top_strip_kernel(bricks, *refs):
    planes, _, across = refs[3].shape

    @pl.when(lax.axis_index("strip") == 0)
    def _():
        shade(bricks, jnp.zeros((planes, across), jnp.float32), *refs)


def other_strips_kernel(bricks, *refs):
    *refs, row_above, top_words_ref, out_ref = refs

    @pl.when(lax.axis_index("strip") == 0)
    def _():
        out_ref[...] = top_words_ref[...]

    @pl.when(lax.axis_index("strip") > 0)
    def _():
        shade(bricks, row_above[...].astype(jnp.float32), *refs, out_ref)


def merge_kernel(planes, before_ref, words_ref, out_ref):
    bricks, _, rows, _ = words_ref.shape
    f32 = jnp.float32
    depth_unit = depth_scale(planes, planes * bricks) / CODE_MAX
    depth, codes = [], []
    for b in range(bricks):
        low, high = words_ref[b, 0], words_ref[b, 1]
        depth.append((low & 0xFFFF).astype(f32) * depth_unit)
        codes.append(
            [lax.shift_right_logical(low, 16), high & 0xFFFF, lax.shift_right_logical(high, 16)]
        )
    colour = [jnp.zeros((rows, LANES), f32)] * 3
    for b in range(bricks):
        base = jnp.full((rows, LANES), COLOUR_LOW, f32)
        for other in range(bricks):
            if other != b:
                base = base - before_ref[b, other : other + 1, :] * depth[other]
        for c in range(3):
            term = jnp.exp2(codes[b][c].astype(f32) * (1.0 / COLOUR_STEPS) + base)
            colour[c] = colour[c] + jnp.where(codes[b][c] > 0, term, 0.0)
    image = colour + [jnp.exp2(-sum(depth))]
    for c in range(4):
        out_ref[pl.ds(c, rows, stride=4), :] = image[c]


def call(kernel, out_shape, *operands, spaces=None, scratch=()):
    vmem = pl.BlockSpec(memory_space=pltpu.VMEM)
    spaces = spaces or {}
    return pl.pallas_call(
        kernel,
        out_shape=out_shape,
        in_specs=[
            pl.BlockSpec(memory_space=spaces.get(i, pltpu.VMEM)) for i in range(len(operands))
        ],
        out_specs=jax.tree.map(lambda _: vmem, out_shape),
        scratch_shapes=scratch,
        compiler_params=pltpu.CompilerParams(vmem_limit_bytes=VMEM_BYTES),
    )(*operands)


def per_device(density, tf_bins, tf_table, brick_order):
    planes, height, across = density.shape
    bricks = lax.axis_size("depth")
    owned = height * across // bricks
    shape = jax.ShapeDtypeStruct
    plane = shape((1, height, across), density.dtype)
    rows = shape((planes, across), density.dtype)
    arguments = [
        pltpu.with_memory_space_constraint(argument, pltpu.HBM)
        for argument in (density, tf_bins, tf_table, brick_order)
    ]
    density, bins, table, order, plane_near, plane_far, row_tail, row_head = call(
        edges_kernel,
        [
            shape(density.shape, density.dtype),
            shape(tf_bins.shape, tf_bins.dtype),
            shape((tf_table.shape[0], LANES), tf_table.dtype),
            shape(brick_order.shape, brick_order.dtype),
            plane,
            plane,
            rows,
            rows,
        ],
        *arguments,
        spaces={i: pltpu.HBM for i in range(4)},
        scratch=[pltpu.VMEM(tf_table.shape, tf_table.dtype), pltpu.SemaphoreType.DMA((4,))],
    )
    plane_far = swap_planes(plane_far, 1)
    plane_near = swap_planes(plane_near, 0)
    row_below = rotate_rows(row_head, -1)
    row_above = rotate_rows(row_tail, 1)
    sheared = shape((planes, 3, height, across), jnp.float32)
    first, second, depth, before = call(
        functools.partial(light_kernel, bricks),
        [
            sheared,
            sheared,
            shape((height, across), jnp.int32),
            shape((bricks, bricks, LANES), jnp.float32),
        ],
        arguments[1],
        bins,
        density,
        table,
        order,
        spaces={0: pltpu.HBM},
        scratch=[pltpu.VMEM(tf_bins.shape, tf_bins.dtype), pltpu.SemaphoreType.DMA],
    )
    words_shape = shape((bricks, 2, owned // LANES, LANES), jnp.int32)
    operands = (plane_far, plane_near, row_below, density, first, second, depth)
    words = call(functools.partial(top_strip_kernel, bricks), words_shape, *operands)
    words = call(
        functools.partial(other_strips_kernel, bricks), words_shape, *operands, row_above, words
    )
    words = lax.all_to_all(words, "depth", 0, 0, tiled=True)
    pieces = owned // LANES
    image = call(
        functools.partial(merge_kernel, planes),
        shape((pieces * 4, LANES), jnp.float32),
        before,
        words,
    )
    return image.reshape(pieces, 4, LANES).transpose(1, 0, 2).reshape(4, owned)


def solution(mesh):
    in_specs = (P("depth", "strip", None), P("depth", "strip", None), P(), P("strip", None))
    out_specs = P(None, ("strip", "depth"))
    return jax.shard_map(
        per_device, mesh=mesh, in_specs=in_specs, out_specs=out_specs, check_vma=False
    )
```

```python
import functools

import jax
import jax.numpy as jnp
from jax import lax
from jax.experimental import pallas as pl
from jax.experimental.pallas import tpu as pltpu
from jax.sharding import PartitionSpec as P

LIGHT = (0.36, 0.48, 0.8)
SHADE_GAIN = 1.5
LOG2E = 1.4426950408889634
LANES = 128
VMEM_BYTES = 8 * 1024 * 1024

MAX_DENSITY = 6.0
MAX_LOOKED = 2.0

COLOUR_STEPS = 2048.0
COLOUR_LOW = -28.0
CODE_MAX = 65535.0


def depth_scale(planes, total_planes):
    return MAX_LOOKED * (1.0 + MAX_DENSITY * MAX_DENSITY) * LOG2E * planes / total_planes


def pairs(count, start):
    swaps = []
    for i in range(start, count - 1, 2):
        swaps += [(i, i + 1), (i + 1, i)]
    return swaps


def partner_exists(index, count, start):
    lower = index % 2 == start
    return jnp.where(lower, index + 1 < count, index > 0)


def edges_kernel(
    density_hbm,
    bins_hbm,
    table_hbm,
    order_hbm,
    density_ref,
    bins_ref,
    table_ref,
    order_ref,
    plane_near,
    plane_far,
    row_tail,
    row_head,
    small_ref,
    semaphores,
):
    density_copy = pltpu.make_async_copy(density_hbm, density_ref, semaphores.at[0])
    density_copy.start()
    odd_strip = lax.axis_index("strip") % 2 == 1

    @pl.when(odd_strip)
    def _():
        pltpu.make_async_copy(bins_hbm, bins_ref, semaphores.at[1]).start()

    table_copy = pltpu.make_async_copy(table_hbm, small_ref, semaphores.at[2])
    order_copy = pltpu.make_async_copy(order_hbm, order_ref, semaphores.at[3])
    table_copy.start()
    order_copy.start()
    table_ref[...] = jnp.zeros_like(table_ref)
    planes, height, _ = density_ref.shape
    odd_brick = lax.axis_index("depth") % 2
    density_copy.wait()
    plane_near[...] = density_ref[pl.ds((1 - odd_brick) * (planes - 1), 1)]
    plane_far[...] = density_ref[pl.ds(odd_brick * (planes - 1), 1)]
    wide = [density_ref[p].astype(jnp.float32) for p in range(planes)]
    tails = jnp.concatenate([rows[height - 1 : height, :] for rows in wide], axis=0)
    heads = jnp.concatenate([rows[0:1, :] for rows in wide], axis=0)
    row_tail[...] = tails.astype(row_tail.dtype)
    row_head[...] = heads.astype(row_head.dtype)
    table_copy.wait()
    table_ref[:, : small_ref.shape[1]] = small_ref[...]
    order_copy.wait()

    @pl.when(odd_strip)
    def _():
        pltpu.make_async_copy(bins_hbm, bins_ref, semaphores.at[1]).wait()


def swap_planes(cells, start):
    bricks, strips = lax.axis_size("depth"), lax.axis_size("strip")
    swaps = pairs(bricks, start)
    links = [((a, s), (b, s)) for a, b in swaps for s in range(strips)]
    if strips % 2 == 0:
        spare = [i for i in range(bricks) if i not in dict(swaps)]
        links += [((a, s), (a, s ^ 1)) for a in spare for s in range(strips)]
    flat = [(a * strips + s, b * strips + t) for (a, s), (b, t) in links]
    return lax.ppermute(cells, ("depth", "strip"), flat)


def rotate_rows(cells, step):
    strips = lax.axis_size("strip")
    return lax.ppermute(cells, "strip", [(i, (i + step) % strips) for i in range(strips)])


def masked(cells, axis, start):
    exists = partner_exists(lax.axis_index(axis), lax.axis_size(axis), start)
    return jnp.where(exists, cells, 0.0)


def tiles_of(value):
    return [value[:, t : t + LANES] for t in range(0, value.shape[1], LANES)]


def lane_next(tiles, lane):
    rolled = [pltpu.roll(v, LANES - 1, 1) for v in tiles] + [0.0]
    return [jnp.where(lane < LANES - 1, rolled[t], rolled[t + 1]) for t in range(len(tiles))]


def lane_previous(tiles, lane):
    rolled = [0.0] + [pltpu.roll(v, 1, 1) for v in tiles]
    return [jnp.where(lane > 0, rolled[t + 1], rolled[t]) for t in range(len(tiles))]


def lane_shift(tiles, lane, shift, beyond):
    amount = (LANES - shift) % LANES
    rolled = [pltpu.roll(v, amount, 1) for v in tiles] + [beyond]
    return [jnp.where(lane < LANES - shift, rolled[t], rolled[t + 1]) for t in range(len(tiles))]


def slopes_across(density_ref, across_ref):
    planes, height, across = density_ref.shape
    lane = lax.broadcasted_iota(jnp.int32, (height, LANES), 1)
    for p in range(planes):
        centre = tiles_of(density_ref[p].astype(jnp.float32))
        ahead, behind = lane_next(centre, lane), lane_previous(centre, lane)
        for t in range(across // LANES):
            across_ref[p, :, t * LANES : (t + 1) * LANES] = ahead[t] - behind[t]


def light_kernel(bricks, bins_hbm, bins_vmem, *refs):
    *refs, across_ref, bins_scratch, semaphore = refs
    odd_strip = lax.axis_index("strip") % 2 == 1

    @pl.when(odd_strip)
    def _():
        slopes_across(refs[0], across_ref)
        light(bricks, bins_vmem, *refs)

    @pl.when(jnp.logical_not(odd_strip))
    def _():
        bins_copy = pltpu.make_async_copy(bins_hbm, bins_scratch, semaphore)
        bins_copy.start()
        slopes_across(refs[0], across_ref)
        bins_copy.wait()
        light(bricks, bins_scratch, *refs)


def light(
    bricks,
    bins_ref,
    density_ref,
    table_ref,
    order_ref,
    first_ref,
    second_ref,
    depth_ref,
    before_ref,
):
    planes, height, across = density_ref.shape
    total_planes = planes * bricks
    count = across // LANES
    f32 = jnp.float32
    lane = lax.broadcasted_iota(jnp.int32, (height, LANES), 1)
    codes = (table_ref[...] * (CODE_MAX / MAX_LOOKED) + 0.5).astype(jnp.int32)
    table = [
        jnp.broadcast_to(codes[c : c + 1, :] | (codes[c + 1 : c + 2, :] << 16), (height, LANES))
        for c in (0, 2)
    ]
    colour_unit = MAX_LOOKED / CODE_MAX
    extinction_unit = colour_unit * LOG2E / total_planes
    depth = [jnp.zeros((height, LANES), f32)] * count
    for p in range(planes):
        plane_index = lax.axis_index("depth") * planes + p
        shift = (3 * plane_index) // 8
        fraction = ((3 * plane_index) % 8).astype(f32) / 8.0
        cells = lane_shift(tiles_of(density_ref[p].astype(f32)), lane, shift, 0.0)
        bins = lane_shift(tiles_of(bins_ref[p]), lane, shift, LANES - 1)
        fields = [[], [], [], []]
        for t in range(count):
            looked = []
            for entry in table:
                word = jnp.take_along_axis(entry, bins[t], axis=1, mode="promise_in_bounds")
                looked += [(word & 0xFFFF).astype(f32), lax.shift_right_logical(word, 16).astype(f32)]
            extinction = looked[0] * (extinction_unit + extinction_unit * (cells[t] * cells[t]))
            opacity = colour_unit - colour_unit * jnp.exp2(-extinction)
            fields[0].append(extinction)
            for c in range(3):
                fields[c + 1].append(looked[c + 1] * opacity)
        after = [lane_next(field, lane) for field in fields]
        for t in range(count):
            cols = slice(t * LANES, (t + 1) * LANES)
            through = jnp.exp2(-depth[t])
            through_second = through * fraction
            through_first = through - through_second
            for c in range(3):
                first_ref[p, c, :, cols] = through_first * fields[c + 1][t]
                second_ref[p, c, :, cols] = through_second * after[c + 1][t]
            depth[t] = depth[t] + (
                fields[0][t] + fraction * (after[0][t] - fields[0][t])
            )
    depth_factor = CODE_MAX / depth_scale(planes, total_planes)
    for t in range(count):
        code = jnp.minimum(depth[t] * depth_factor, CODE_MAX)
        depth_ref[:, t * LANES : (t + 1) * LANES] = (code + 0.5).astype(jnp.int32)
    slot = lax.broadcasted_iota(jnp.int32, (bricks, LANES), 0)
    place = jnp.zeros((bricks, LANES), jnp.int32)
    for k in range(bricks):
        brick = jnp.broadcast_to(order_ref[0:1, k : k + 1], (bricks, LANES))
        place = jnp.where(slot == brick, k, place)
    for b in range(bricks):
        before_ref[b] = (place < place[b : b + 1, :]).astype(f32)


def shade(
    bricks,
    above,
    plane_far,
    plane_near,
    row_below,
    density_ref,
    first_ref,
    second_ref,
    depth_ref,
    across_ref,
    out_ref,
):
    planes, height, across = density_ref.shape
    count = across // LANES
    f32 = jnp.float32
    odd_brick = lax.axis_index("depth") % 2 == 1
    lane = lax.broadcasted_iota(jnp.int32, (height, LANES), 1)
    row = lax.broadcasted_iota(jnp.int32, (height, LANES), 0)
    near = masked(plane_near[0].astype(f32), "depth", 0)
    far = masked(plane_far[0].astype(f32), "depth", 1)
    beneath = tiles_of(jnp.where(odd_brick, near, far))
    overhead = tiles_of(jnp.where(odd_brick, far, near))
    strip = lax.axis_index("strip")
    below = jnp.where(strip < lax.axis_size("strip") - 1, row_below[...].astype(f32), 0.0)
    stack = [beneath]
    stack += [tiles_of(density_ref[p].astype(f32)) for p in range(planes)]
    stack += [overhead]
    gain = SHADE_GAIN * LOG2E
    colour = [[None] * count for _ in range(3)]
    for p in range(planes):
        shift = (3 * (lax.axis_index("depth") * planes + p)) // 8
        centre = stack[p + 1]
        shade = []
        for t in range(count):
            cols = slice(t * LANES, (t + 1) * LANES)
            v = centre[t]
            up = jnp.where(row == 0, above[p : p + 1, cols], pltpu.roll(v, 1, 0))
            down = jnp.where(
                row == height - 1, below[p : p + 1, cols], pltpu.roll(v, height - 1, 0)
            )
            dx = across_ref[p, :, cols]
            dy = down - up
            dz = stack[p + 2][t] - stack[p][t]
            lit = (LIGHT[0] * gain) * dx + (LIGHT[1] * gain) * dy + (LIGHT[2] * gain) * dz
            shade.append(jnp.exp2(lit * lax.rsqrt(4.0 + dx * dx + dy * dy + dz * dz)))
        shade = lane_shift(shade, lane, shift, 0.0)
        after = lane_next(shade, lane)
        for t in range(count):
            cols = slice(t * LANES, (t + 1) * LANES)
            for c in range(3):
                term = first_ref[p, c, :, cols] * shade[t] + second_ref[p, c, :, cols] * after[t]
                colour[c][t] = term if p == 0 else colour[c][t] + term

    words = [[], []]
    for t in range(count):
        codes = [depth_ref[:, t * LANES : (t + 1) * LANES]]
        for c in range(3):
            code = jnp.log2(colour[c][t]) * COLOUR_STEPS + (0.5 - COLOUR_LOW * COLOUR_STEPS)
            codes.append(jnp.minimum(jnp.maximum(code, 0.0), CODE_MAX).astype(jnp.int32))
        words[0].append(codes[0] | (codes[1] << 16))
        words[1].append(codes[2] | (codes[3] << 16))
    owned = height * across // bricks
    tall, wide = max(owned // across, 1), min(owned, across)
    for owner in range(bricks):
        top, left = owner * owned // across, owner * owned % across
        for w in range(2):
            for t in range(wide // LANES):
                for r in range(tall):
                    out_ref[owner, w, r * (wide // LANES) + t : r * (wide // LANES) + t + 1, :] = words[
                        w
                    ][left // LANES + t][top + r : top + r + 1, :]


def top_strip_kernel(bricks, *refs):
    planes, _, across = refs[3].shape

    @pl.when(lax.axis_index("strip") == 0)
    def _():
        shade(bricks, jnp.zeros((planes, across), jnp.float32), *refs)


def other_strips_kernel(bricks, *refs):
    *refs, row_above, top_words_ref, out_ref = refs

    @pl.when(lax.axis_index("strip") == 0)
    def _():
        out_ref[...] = top_words_ref[...]

    @pl.when(lax.axis_index("strip") > 0)
    def _():
        shade(bricks, row_above[...].astype(jnp.float32), *refs, out_ref)


def merge_kernel(planes, before_ref, words_ref, out_ref):
    bricks, _, rows, _ = words_ref.shape
    f32 = jnp.float32
    depth_unit = depth_scale(planes, planes * bricks) / CODE_MAX
    depth, codes = [], []
    for b in range(bricks):
        low, high = words_ref[b, 0], words_ref[b, 1]
        depth.append((low & 0xFFFF).astype(f32) * depth_unit)
        codes.append(
            [lax.shift_right_logical(low, 16), high & 0xFFFF, lax.shift_right_logical(high, 16)]
        )
    colour = [jnp.zeros((rows, LANES), f32)] * 3
    for b in range(bricks):
        base = jnp.full((rows, LANES), COLOUR_LOW, f32)
        for other in range(bricks):
            if other != b:
                base = base - before_ref[b, other : other + 1, :] * depth[other]
        for c in range(3):
            term = jnp.exp2(codes[b][c].astype(f32) * (1.0 / COLOUR_STEPS) + base)
            colour[c] = colour[c] + jnp.where(codes[b][c] > 0, term, 0.0)
    image = colour + [jnp.exp2(-sum(depth))]
    for c in range(4):
        out_ref[pl.ds(c, rows, stride=4), :] = image[c]


def call(kernel, out_shape, *operands, spaces=None, scratch=()):
    vmem = pl.BlockSpec(memory_space=pltpu.VMEM)
    spaces = spaces or {}
    return pl.pallas_call(
        kernel,
        out_shape=out_shape,
        in_specs=[
            pl.BlockSpec(memory_space=spaces.get(i, pltpu.VMEM)) for i in range(len(operands))
        ],
        out_specs=jax.tree.map(lambda _: vmem, out_shape),
        scratch_shapes=scratch,
        compiler_params=pltpu.CompilerParams(vmem_limit_bytes=VMEM_BYTES),
    )(*operands)


def per_device(density, tf_bins, tf_table, brick_order):
    planes, height, across = density.shape
    bricks = lax.axis_size("depth")
    owned = height * across // bricks
    shape = jax.ShapeDtypeStruct
    plane = shape((1, height, across), density.dtype)
    rows = shape((planes, across), density.dtype)
    arguments = [
        pltpu.with_memory_space_constraint(argument, pltpu.HBM)
        for argument in (density, tf_bins, tf_table, brick_order)
    ]
    density, bins, table, order, plane_near, plane_far, row_tail, row_head = call(
        edges_kernel,
        [
            shape(density.shape, density.dtype),
            shape(tf_bins.shape, tf_bins.dtype),
            shape((tf_table.shape[0], LANES), tf_table.dtype),
            shape(brick_order.shape, brick_order.dtype),
            plane,
            plane,
            rows,
            rows,
        ],
        *arguments,
        spaces={i: pltpu.HBM for i in range(4)},
        scratch=[pltpu.VMEM(tf_table.shape, tf_table.dtype), pltpu.SemaphoreType.DMA((4,))],
    )
    plane_far = swap_planes(plane_far, 1)
    plane_near = swap_planes(plane_near, 0)
    row_below = rotate_rows(row_head, -1)
    row_above = rotate_rows(row_tail, 1)
    sheared = shape((planes, 3, height, across), jnp.float32)
    first, second, depth, before, across_slopes = call(
        functools.partial(light_kernel, bricks),
        [
            sheared,
            sheared,
            shape((height, across), jnp.int32),
            shape((bricks, bricks, LANES), jnp.float32),
            shape((planes, height, across), jnp.float32),
        ],
        arguments[1],
        bins,
        density,
        table,
        order,
        spaces={0: pltpu.HBM},
        scratch=[pltpu.VMEM(tf_bins.shape, tf_bins.dtype), pltpu.SemaphoreType.DMA],
    )
    words_shape = shape((bricks, 2, owned // LANES, LANES), jnp.int32)
    operands = (plane_far, plane_near, row_below, density, first, second, depth, across_slopes)
    words = call(functools.partial(top_strip_kernel, bricks), words_shape, *operands)
    words = call(
        functools.partial(other_strips_kernel, bricks), words_shape, *operands, row_above, words
    )
    words = lax.all_to_all(words, "depth", 0, 0, tiled=True)
    pieces = owned // LANES
    image = call(
        functools.partial(merge_kernel, planes),
        shape((pieces * 4, LANES), jnp.float32),
        before,
        words,
    )
    return image.reshape(pieces, 4, LANES).transpose(1, 0, 2).reshape(4, owned)


def solution(mesh):
    in_specs = (P("depth", "strip", None), P("depth", "strip", None), P(), P("strip", None))
    out_specs = P(None, ("strip", "depth"))
    return jax.shard_map(
        per_device, mesh=mesh, in_specs=in_specs, out_specs=out_specs, check_vma=False
    )
```

```python
import functools

import jax
import jax.numpy as jnp
from jax import lax
from jax.experimental import pallas as pl
from jax.experimental.pallas import tpu as pltpu
from jax.sharding import PartitionSpec as P

LIGHT = (0.36, 0.48, 0.8)
SHADE_GAIN = 1.5
LOG2E = 1.4426950408889634
LANES = 128
VMEM_BYTES = 8 * 1024 * 1024

MAX_DENSITY = 6.0
MAX_LOOKED = 2.0

COLOUR_STEPS = 2048.0
COLOUR_LOW = -28.0
CODE_MAX = 65535.0


def depth_scale(planes, total_planes):
    return MAX_LOOKED * (1.0 + MAX_DENSITY * MAX_DENSITY) * LOG2E * planes / total_planes


def pairs(count, start):
    swaps = []
    for i in range(start, count - 1, 2):
        swaps += [(i, i + 1), (i + 1, i)]
    return swaps


def partner_exists(index, count, start):
    lower = index % 2 == start
    return jnp.where(lower, index + 1 < count, index > 0)


def edges_kernel(
    density_hbm,
    bins_hbm,
    table_hbm,
    order_hbm,
    density_ref,
    bins_ref,
    table_ref,
    order_ref,
    plane_near,
    plane_far,
    row_tail,
    row_head,
    small_ref,
    semaphores,
):
    density_copy = pltpu.make_async_copy(density_hbm, density_ref, semaphores.at[0])
    density_copy.start()
    odd_strip = lax.axis_index("strip") % 2 == 1

    @pl.when(odd_strip)
    def _():
        pltpu.make_async_copy(bins_hbm, bins_ref, semaphores.at[1]).start()

    table_copy = pltpu.make_async_copy(table_hbm, small_ref, semaphores.at[2])
    order_copy = pltpu.make_async_copy(order_hbm, order_ref, semaphores.at[3])
    table_copy.start()
    order_copy.start()
    table_ref[...] = jnp.zeros_like(table_ref)
    planes, height, _ = density_ref.shape
    odd_brick = lax.axis_index("depth") % 2
    density_copy.wait()
    plane_near[...] = density_ref[pl.ds((1 - odd_brick) * (planes - 1), 1)]
    plane_far[...] = density_ref[pl.ds(odd_brick * (planes - 1), 1)]
    wide = [density_ref[p].astype(jnp.float32) for p in range(planes)]
    tails = jnp.concatenate([rows[height - 1 : height, :] for rows in wide], axis=0)
    heads = jnp.concatenate([rows[0:1, :] for rows in wide], axis=0)
    row_tail[...] = tails.astype(row_tail.dtype)
    row_head[...] = heads.astype(row_head.dtype)
    table_copy.wait()
    table_ref[:, : small_ref.shape[1]] = small_ref[...]
    order_copy.wait()

    @pl.when(odd_strip)
    def _():
        pltpu.make_async_copy(bins_hbm, bins_ref, semaphores.at[1]).wait()


def swap_planes(cells, start):
    bricks, strips = lax.axis_size("depth"), lax.axis_size("strip")
    swaps = pairs(bricks, start)
    links = [((a, s), (b, s)) for a, b in swaps for s in range(strips)]
    if strips % 2 == 0:
        spare = [i for i in range(bricks) if i not in dict(swaps)]
        links += [((a, s), (a, s ^ 1)) for a in spare for s in range(strips)]
    flat = [(a * strips + s, b * strips + t) for (a, s), (b, t) in links]
    return lax.ppermute(cells, ("depth", "strip"), flat)


def rotate_rows(cells, step):
    strips = lax.axis_size("strip")
    return lax.ppermute(cells, "strip", [(i, (i + step) % strips) for i in range(strips)])


def masked(cells, axis, start):
    exists = partner_exists(lax.axis_index(axis), lax.axis_size(axis), start)
    return jnp.where(exists, cells, 0.0)


def tiles_of(value):
    return [value[:, t : t + LANES] for t in range(0, value.shape[1], LANES)]


def lane_next(tiles, lane):
    rolled = [pltpu.roll(v, LANES - 1, 1) for v in tiles] + [0.0]
    return [jnp.where(lane < LANES - 1, rolled[t], rolled[t + 1]) for t in range(len(tiles))]


def lane_previous(tiles, lane):
    rolled = [0.0] + [pltpu.roll(v, 1, 1) for v in tiles]
    return [jnp.where(lane > 0, rolled[t + 1], rolled[t]) for t in range(len(tiles))]


def lane_shift(tiles, lane, shift, beyond):
    amount = (LANES - shift) % LANES
    rolled = [pltpu.roll(v, amount, 1) for v in tiles] + [beyond]
    return [jnp.where(lane < LANES - shift, rolled[t], rolled[t + 1]) for t in range(len(tiles))]


def light_kernel(bricks, bins_hbm, bins_vmem, *refs):
    *refs, bins_scratch, semaphore = refs
    odd_strip = lax.axis_index("strip") % 2 == 1

    @pl.when(odd_strip)
    def _():
        light(bricks, bins_vmem, *refs)

    @pl.when(jnp.logical_not(odd_strip))
    def _():
        bins_copy = pltpu.make_async_copy(bins_hbm, bins_scratch, semaphore)
        bins_copy.start()
        bins_copy.wait()
        light(bricks, bins_scratch, *refs)


def light(
    bricks,
    bins_ref,
    density_ref,
    table_ref,
    order_ref,
    first_ref,
    second_ref,
    depth_ref,
    before_ref,
):
    planes, height, across = density_ref.shape
    total_planes = planes * bricks
    count = across // LANES
    f32 = jnp.float32
    lane = lax.broadcasted_iota(jnp.int32, (height, LANES), 1)
    codes = (table_ref[...] * (CODE_MAX / MAX_LOOKED) + 0.5).astype(jnp.int32)
    table = [
        jnp.broadcast_to(codes[c : c + 1, :] | (codes[c + 1 : c + 2, :] << 16), (height, LANES))
        for c in (0, 2)
    ]
    colour_unit = MAX_LOOKED / CODE_MAX
    extinction_unit = colour_unit * LOG2E / total_planes
    depth = [jnp.zeros((height, LANES), f32)] * count
    for p in range(planes):
        plane_index = lax.axis_index("depth") * planes + p
        shift = (3 * plane_index) // 8
        fraction = ((3 * plane_index) % 8).astype(f32) / 8.0
        cells = lane_shift(tiles_of(density_ref[p].astype(f32)), lane, shift, 0.0)
        bins = lane_shift(tiles_of(bins_ref[p]), lane, shift, LANES - 1)
        fields = [[], [], [], []]
        for t in range(count):
            looked = []
            for entry in table:
                word = jnp.take_along_axis(entry, bins[t], axis=1, mode="promise_in_bounds")
                looked += [(word & 0xFFFF).astype(f32), lax.shift_right_logical(word, 16).astype(f32)]
            extinction = looked[0] * (extinction_unit + extinction_unit * (cells[t] * cells[t]))
            opacity = colour_unit - colour_unit * jnp.exp2(-extinction)
            fields[0].append(extinction)
            for c in range(3):
                fields[c + 1].append(looked[c + 1] * opacity)
        after = [lane_next(field, lane) for field in fields]
        for t in range(count):
            cols = slice(t * LANES, (t + 1) * LANES)
            through = jnp.exp2(-depth[t])
            through_second = through * fraction
            through_first = through - through_second
            for c in range(3):
                first_ref[p, c, :, cols] = through_first * fields[c + 1][t]
                second_ref[p, c, :, cols] = through_second * after[c + 1][t]
            depth[t] = depth[t] + (
                fields[0][t] + fraction * (after[0][t] - fields[0][t])
            )
    depth_factor = CODE_MAX / depth_scale(planes, total_planes)
    for t in range(count):
        code = jnp.minimum(depth[t] * depth_factor, CODE_MAX)
        depth_ref[:, t * LANES : (t + 1) * LANES] = (code + 0.5).astype(jnp.int32)
    slot = lax.broadcasted_iota(jnp.int32, (bricks, LANES), 0)
    place = jnp.zeros((bricks, LANES), jnp.int32)
    for k in range(bricks):
        brick = jnp.broadcast_to(order_ref[0:1, k : k + 1], (bricks, LANES))
        place = jnp.where(slot == brick, k, place)
    for b in range(bricks):
        before_ref[b] = (place < place[b : b + 1, :]).astype(f32)


def shade(
    bricks,
    above,
    plane_far,
    plane_near,
    row_below,
    density_ref,
    first_ref,
    second_ref,
    depth_ref,
    out_ref,
):
    planes, height, across = density_ref.shape
    count = across // LANES
    f32 = jnp.float32
    odd_brick = lax.axis_index("depth") % 2 == 1
    lane = lax.broadcasted_iota(jnp.int32, (height, LANES), 1)
    row = lax.broadcasted_iota(jnp.int32, (height, LANES), 0)
    near = masked(plane_near[0].astype(f32), "depth", 0)
    far = masked(plane_far[0].astype(f32), "depth", 1)
    beneath = tiles_of(jnp.where(odd_brick, near, far))
    overhead = tiles_of(jnp.where(odd_brick, far, near))
    strip = lax.axis_index("strip")
    below = jnp.where(strip < lax.axis_size("strip") - 1, row_below[...].astype(f32), 0.0)
    stack = [beneath]
    stack += [tiles_of(density_ref[p].astype(f32)) for p in range(planes)]
    stack += [overhead]
    gain = SHADE_GAIN * LOG2E
    colour = [[None] * count for _ in range(3)]
    for p in range(planes):
        shift = (3 * (lax.axis_index("depth") * planes + p)) // 8
        centre = stack[p + 1]
        ahead, behind = lane_next(centre, lane), lane_previous(centre, lane)
        shade = []
        for t in range(count):
            cols = slice(t * LANES, (t + 1) * LANES)
            v = centre[t]
            up = jnp.where(row == 0, above[p : p + 1, cols], pltpu.roll(v, 1, 0))
            down = jnp.where(
                row == height - 1, below[p : p + 1, cols], pltpu.roll(v, height - 1, 0)
            )
            dx = ahead[t] - behind[t]
            dy = down - up
            dz = stack[p + 2][t] - stack[p][t]
            lit = (LIGHT[0] * gain) * dx + (LIGHT[1] * gain) * dy + (LIGHT[2] * gain) * dz
            shade.append(jnp.exp2(lit * lax.rsqrt(4.0 + dx * dx + dy * dy + dz * dz)))
        shade = lane_shift(shade, lane, shift, 0.0)
        after = lane_next(shade, lane)
        for t in range(count):
            cols = slice(t * LANES, (t + 1) * LANES)
            for c in range(3):
                term = first_ref[p, c, :, cols] * shade[t] + second_ref[p, c, :, cols] * after[t]
                colour[c][t] = term if p == 0 else colour[c][t] + term

    words = [[], []]
    for t in range(count):
        codes = [depth_ref[:, t * LANES : (t + 1) * LANES]]
        for c in range(3):
            code = jnp.log2(colour[c][t]) * COLOUR_STEPS + (0.5 - COLOUR_LOW * COLOUR_STEPS)
            codes.append(jnp.minimum(jnp.maximum(code, 0.0), CODE_MAX).astype(jnp.int32))
        words[0].append(codes[0] | (codes[1] << 16))
        words[1].append(codes[2] | (codes[3] << 16))
    owned = height * across // bricks
    tall, wide = max(owned // across, 1), min(owned, across)
    for owner in range(bricks):
        top, left = owner * owned // across, owner * owned % across
        for w in range(2):
            for t in range(wide // LANES):
                out_ref[owner, w, t * tall : (t + 1) * tall, :] = words[w][left // LANES + t][
                    top : top + tall, :
                ]


def top_strip_kernel(bricks, *refs):
    planes, _, across = refs[3].shape

    @pl.when(lax.axis_index("strip") == 0)
    def _():
        shade(bricks, jnp.zeros((planes, across), jnp.float32), *refs)


def other_strips_kernel(bricks, *refs):
    *refs, row_above, top_words_ref, out_ref = refs

    @pl.when(lax.axis_index("strip") == 0)
    def _():
        out_ref[...] = top_words_ref[...]

    @pl.when(lax.axis_index("strip") > 0)
    def _():
        shade(bricks, row_above[...].astype(jnp.float32), *refs, out_ref)


def merge_kernel(planes, tall, before_ref, words_ref, out_ref):
    bricks, _, rows, _ = words_ref.shape
    f32 = jnp.float32
    depth_unit = depth_scale(planes, planes * bricks) / CODE_MAX
    depth, codes = [], []
    for b in range(bricks):
        low, high = words_ref[b, 0], words_ref[b, 1]
        depth.append((low & 0xFFFF).astype(f32) * depth_unit)
        codes.append(
            [lax.shift_right_logical(low, 16), high & 0xFFFF, lax.shift_right_logical(high, 16)]
        )
    colour = [jnp.zeros((rows, LANES), f32)] * 3
    for b in range(bricks):
        base = jnp.full((rows, LANES), COLOUR_LOW, f32)
        for other in range(bricks):
            if other != b:
                base = base - before_ref[b, other : other + 1, :] * depth[other]
        for c in range(3):
            term = jnp.exp2(codes[b][c].astype(f32) * (1.0 / COLOUR_STEPS) + base)
            colour[c] = colour[c] + jnp.where(codes[b][c] > 0, term, 0.0)
    image = colour + [jnp.exp2(-sum(depth))]
    wide = rows // tall
    for c in range(4):
        for r in range(tall):
            for t in range(wide):
                at = (r * wide + t) * LANES
                out_ref[c : c + 1, at : at + LANES] = image[c][t * tall + r : t * tall + r + 1, :]


def call(kernel, out_shape, *operands, spaces=None, scratch=(), aliases=None):
    vmem = pl.BlockSpec(memory_space=pltpu.VMEM)
    spaces = spaces or {}
    return pl.pallas_call(
        kernel,
        out_shape=out_shape,
        in_specs=[
            pl.BlockSpec(memory_space=spaces.get(i, pltpu.VMEM)) for i in range(len(operands))
        ],
        out_specs=jax.tree.map(lambda _: vmem, out_shape),
        scratch_shapes=scratch,
        input_output_aliases=aliases or {},
        compiler_params=pltpu.CompilerParams(vmem_limit_bytes=VMEM_BYTES),
    )(*operands)


def per_device(density, tf_bins, tf_table, brick_order):
    planes, height, across = density.shape
    bricks = lax.axis_size("depth")
    owned = height * across // bricks
    shape = jax.ShapeDtypeStruct
    plane = shape((1, height, across), density.dtype)
    rows = shape((planes, across), density.dtype)
    arguments = [
        pltpu.with_memory_space_constraint(argument, pltpu.HBM)
        for argument in (density, tf_bins, tf_table, brick_order)
    ]
    density, bins, table, order, plane_near, plane_far, row_tail, row_head = call(
        edges_kernel,
        [
            shape(density.shape, density.dtype),
            shape(tf_bins.shape, tf_bins.dtype),
            shape((tf_table.shape[0], LANES), tf_table.dtype),
            shape(brick_order.shape, brick_order.dtype),
            plane,
            plane,
            rows,
            rows,
        ],
        *arguments,
        spaces={i: pltpu.HBM for i in range(4)},
        scratch=[pltpu.VMEM(tf_table.shape, tf_table.dtype), pltpu.SemaphoreType.DMA((4,))],
    )
    plane_far = swap_planes(plane_far, 1)
    plane_near = swap_planes(plane_near, 0)
    row_below = rotate_rows(row_head, -1)
    row_above = rotate_rows(row_tail, 1)
    sheared = shape((planes, 3, height, across), jnp.float32)
    first, second, depth, before = call(
        functools.partial(light_kernel, bricks),
        [
            sheared,
            sheared,
            shape((height, across), jnp.int32),
            shape((bricks, bricks, LANES), jnp.float32),
        ],
        arguments[1],
        bins,
        density,
        table,
        order,
        spaces={0: pltpu.HBM},
        scratch=[pltpu.VMEM(tf_bins.shape, tf_bins.dtype), pltpu.SemaphoreType.DMA],
    )
    words_shape = shape((bricks, 2, owned // LANES, LANES), jnp.int32)
    operands = (plane_far, plane_near, row_below, density, first, second, depth)
    words = call(functools.partial(top_strip_kernel, bricks), words_shape, *operands)
    words = call(
        functools.partial(other_strips_kernel, bricks), words_shape, *operands, row_above, words, aliases={8: 0}
    )
    words = lax.all_to_all(words, "depth", 0, 0, tiled=True)
    return call(
        functools.partial(merge_kernel, planes, max(owned // across, 1)),
        shape((4, owned), jnp.float32),
        before,
        words,
    )


def solution(mesh):
    in_specs = (P("depth", "strip", None), P("depth", "strip", None), P(), P("strip", None))
    out_specs = P(None, ("strip", "depth"))
    return jax.shard_map(
        per_device, mesh=mesh, in_specs=in_specs, out_specs=out_specs, check_vma=False
    )
```

```python
import functools

import jax
import jax.numpy as jnp
from jax import lax
from jax.experimental import pallas as pl
from jax.experimental.pallas import tpu as pltpu
from jax.sharding import PartitionSpec as P

LIGHT = (0.36, 0.48, 0.8)
SHADE_GAIN = 1.5
LOG2E = 1.4426950408889634
LANES = 128
VMEM_BYTES = 8 * 1024 * 1024

MAX_DENSITY = 6.0
MAX_LOOKED = 2.0

COLOUR_STEPS = 2048.0
COLOUR_LOW = -28.0
CODE_MAX = 65535.0


def depth_scale(planes, total_planes):
    return MAX_LOOKED * (1.0 + MAX_DENSITY * MAX_DENSITY) * LOG2E * planes / total_planes


def pairs(count, start):
    swaps = []
    for i in range(start, count - 1, 2):
        swaps += [(i, i + 1), (i + 1, i)]
    return swaps


def partner_exists(index, count, start):
    lower = index % 2 == start
    return jnp.where(lower, index + 1 < count, index > 0)


def edges_kernel(
    density_hbm,
    bins_hbm,
    table_hbm,
    order_hbm,
    density_ref,
    bins_ref,
    table_ref,
    order_ref,
    plane_near,
    plane_far,
    row_tail,
    row_head,
    small_ref,
    semaphores,
):
    density_copy = pltpu.make_async_copy(density_hbm, density_ref, semaphores.at[0])
    density_copy.start()
    odd_strip = lax.axis_index("strip") % 2 == 1

    @pl.when(odd_strip)
    def _():
        pltpu.make_async_copy(bins_hbm, bins_ref, semaphores.at[1]).start()

    table_copy = pltpu.make_async_copy(table_hbm, small_ref, semaphores.at[2])
    order_copy = pltpu.make_async_copy(order_hbm, order_ref, semaphores.at[3])
    table_copy.start()
    order_copy.start()
    table_ref[...] = jnp.zeros_like(table_ref)
    planes, height, _ = density_ref.shape
    odd_brick = lax.axis_index("depth") % 2
    density_copy.wait()
    plane_near[...] = density_ref[pl.ds((1 - odd_brick) * (planes - 1), 1)]
    plane_far[...] = density_ref[pl.ds(odd_brick * (planes - 1), 1)]
    wide = [density_ref[p].astype(jnp.float32) for p in range(planes)]
    tails = jnp.concatenate([rows[height - 1 : height, :] for rows in wide], axis=0)
    heads = jnp.concatenate([rows[0:1, :] for rows in wide], axis=0)
    row_tail[...] = tails.astype(row_tail.dtype)
    row_head[...] = heads.astype(row_head.dtype)
    table_copy.wait()
    table_ref[:, : small_ref.shape[1]] = small_ref[...]
    order_copy.wait()

    @pl.when(odd_strip)
    def _():
        pltpu.make_async_copy(bins_hbm, bins_ref, semaphores.at[1]).wait()


def swap_planes(cells, start):
    bricks, strips = lax.axis_size("depth"), lax.axis_size("strip")
    swaps = pairs(bricks, start)
    links = [((a, s), (b, s)) for a, b in swaps for s in range(strips)]
    if strips % 2 == 0:
        spare = [i for i in range(bricks) if i not in dict(swaps)]
        links += [((a, s), (a, s ^ 1)) for a in spare for s in range(strips)]
    flat = [(a * strips + s, b * strips + t) for (a, s), (b, t) in links]
    return lax.ppermute(cells, ("depth", "strip"), flat)


def rotate_rows(cells, step):
    strips = lax.axis_size("strip")
    return lax.ppermute(cells, "strip", [(i, (i + step) % strips) for i in range(strips)])


def masked(cells, axis, start):
    exists = partner_exists(lax.axis_index(axis), lax.axis_size(axis), start)
    return jnp.where(exists, cells, 0.0)


def tiles_of(value):
    return [value[:, t : t + LANES] for t in range(0, value.shape[1], LANES)]


def lane_next(tiles, lane):
    rolled = [pltpu.roll(v, LANES - 1, 1) for v in tiles] + [0.0]
    return [jnp.where(lane < LANES - 1, rolled[t], rolled[t + 1]) for t in range(len(tiles))]


def lane_previous(tiles, lane):
    rolled = [0.0] + [pltpu.roll(v, 1, 1) for v in tiles]
    return [jnp.where(lane > 0, rolled[t + 1], rolled[t]) for t in range(len(tiles))]


def lane_shift(tiles, lane, shift, beyond):
    amount = (LANES - shift) % LANES
    rolled = [pltpu.roll(v, amount, 1) for v in tiles] + [beyond]
    return [jnp.where(lane < LANES - shift, rolled[t], rolled[t + 1]) for t in range(len(tiles))]


def light_kernel(bricks, bins_hbm, bins_vmem, *refs):
    *refs, bins_scratch, semaphore = refs
    odd_strip = lax.axis_index("strip") % 2 == 1

    @pl.when(odd_strip)
    def _():
        light(bricks, bins_vmem, *refs)

    @pl.when(jnp.logical_not(odd_strip))
    def _():
        bins_copy = pltpu.make_async_copy(bins_hbm, bins_scratch, semaphore)
        bins_copy.start()
        bins_copy.wait()
        light(bricks, bins_scratch, *refs)


def light(
    bricks,
    bins_ref,
    density_ref,
    table_ref,
    order_ref,
    first_ref,
    second_ref,
    depth_ref,
    before_ref,
):
    planes, height, across = density_ref.shape
    total_planes = planes * bricks
    count = across // LANES
    f32 = jnp.float32
    lane = lax.broadcasted_iota(jnp.int32, (height, LANES), 1)
    codes = (table_ref[...] * (CODE_MAX / MAX_LOOKED) + 0.5).astype(jnp.int32)
    table = [
        jnp.broadcast_to(codes[c : c + 1, :] | (codes[c + 1 : c + 2, :] << 16), (height, LANES))
        for c in (0, 2)
    ]
    colour_unit = MAX_LOOKED / CODE_MAX
    extinction_unit = colour_unit * LOG2E / total_planes
    depth = [jnp.zeros((height, LANES), f32)] * count
    for p in range(planes):
        plane_index = lax.axis_index("depth") * planes + p
        shift = (3 * plane_index) // 8
        fraction = ((3 * plane_index) % 8).astype(f32) / 8.0
        cells = lane_shift(tiles_of(density_ref[p].astype(f32)), lane, shift, 0.0)
        bins = lane_shift(tiles_of(bins_ref[p]), lane, shift, LANES - 1)
        fields = [[], [], [], []]
        for t in range(count):
            looked = []
            for entry in table:
                word = jnp.take_along_axis(entry, bins[t], axis=1, mode="promise_in_bounds")
                looked += [(word & 0xFFFF).astype(f32), lax.shift_right_logical(word, 16).astype(f32)]
            extinction = looked[0] * (extinction_unit + extinction_unit * (cells[t] * cells[t]))
            opacity = colour_unit - colour_unit * jnp.exp2(-extinction)
            fields[0].append(extinction)
            for c in range(3):
                fields[c + 1].append(looked[c + 1] * opacity)
        after = [lane_next(field, lane) for field in fields]
        for t in range(count):
            cols = slice(t * LANES, (t + 1) * LANES)
            through = jnp.exp2(-depth[t])
            through_second = through * fraction
            through_first = through - through_second
            for c in range(3):
                first_ref[p, c, :, cols] = through_first * fields[c + 1][t]
                second_ref[p, c, :, cols] = through_second * after[c + 1][t]
            depth[t] = depth[t] + (
                fields[0][t] + fraction * (after[0][t] - fields[0][t])
            )
    depth_factor = CODE_MAX / depth_scale(planes, total_planes)
    for t in range(count):
        code = jnp.minimum(depth[t] * depth_factor, CODE_MAX)
        depth_ref[:, t * LANES : (t + 1) * LANES] = (code + 0.5).astype(jnp.int32)
    slot = lax.broadcasted_iota(jnp.int32, (bricks, LANES), 0)
    place = jnp.zeros((bricks, LANES), jnp.int32)
    for k in range(bricks):
        brick = jnp.broadcast_to(order_ref[0:1, k : k + 1], (bricks, LANES))
        place = jnp.where(slot == brick, k, place)
    for b in range(bricks):
        before_ref[b] = (place < place[b : b + 1, :]).astype(f32)


def shade(
    bricks,
    above,
    plane_far,
    plane_near,
    row_below,
    density_ref,
    first_ref,
    second_ref,
    depth_ref,
    out_ref,
):
    planes, height, across = density_ref.shape
    count = across // LANES
    f32 = jnp.float32
    odd_brick = lax.axis_index("depth") % 2 == 1
    lane = lax.broadcasted_iota(jnp.int32, (height, LANES), 1)
    row = lax.broadcasted_iota(jnp.int32, (height, LANES), 0)
    near = masked(plane_near[0].astype(f32), "depth", 0)
    far = masked(plane_far[0].astype(f32), "depth", 1)
    beneath = tiles_of(jnp.where(odd_brick, near, far))
    overhead = tiles_of(jnp.where(odd_brick, far, near))
    strip = lax.axis_index("strip")
    below = jnp.where(strip < lax.axis_size("strip") - 1, row_below[...].astype(f32), 0.0)
    stack = [beneath]
    stack += [tiles_of(density_ref[p].astype(f32)) for p in range(planes)]
    stack += [overhead]
    gain = SHADE_GAIN * LOG2E
    colour = [[None] * count for _ in range(3)]
    for p in range(planes):
        shift = (3 * (lax.axis_index("depth") * planes + p)) // 8
        centre = stack[p + 1]
        ahead, behind = lane_next(centre, lane), lane_previous(centre, lane)
        shade = []
        for t in range(count):
            cols = slice(t * LANES, (t + 1) * LANES)
            v = centre[t]
            up = jnp.where(row == 0, above[p : p + 1, cols], pltpu.roll(v, 1, 0))
            down = jnp.where(
                row == height - 1, below[p : p + 1, cols], pltpu.roll(v, height - 1, 0)
            )
            dx = ahead[t] - behind[t]
            dy = down - up
            dz = stack[p + 2][t] - stack[p][t]
            lit = (LIGHT[0] * gain) * dx + (LIGHT[1] * gain) * dy + (LIGHT[2] * gain) * dz
            shade.append(jnp.exp2(lit * lax.rsqrt(4.0 + dx * dx + dy * dy + dz * dz)))
        shade = lane_shift(shade, lane, shift, 0.0)
        after = lane_next(shade, lane)
        for t in range(count):
            cols = slice(t * LANES, (t + 1) * LANES)
            for c in range(3):
                term = first_ref[p, c, :, cols] * shade[t] + second_ref[p, c, :, cols] * after[t]
                colour[c][t] = term if p == 0 else colour[c][t] + term

    words = [[], []]
    for t in range(count):
        codes = [depth_ref[:, t * LANES : (t + 1) * LANES]]
        for c in range(3):
            code = jnp.log2(colour[c][t]) * COLOUR_STEPS + (0.5 - COLOUR_LOW * COLOUR_STEPS)
            codes.append(jnp.minimum(jnp.maximum(code, 0.0), CODE_MAX).astype(jnp.int32))
        words[0].append(codes[0] | (codes[1] << 16))
        words[1].append(codes[2] | (codes[3] << 16))
    owned = height * across // bricks
    tall, wide = max(owned // across, 1), min(owned, across)
    for owner in range(bricks):
        top, left = owner * owned // across, owner * owned % across
        for w in range(2):
            for t in range(wide // LANES):
                for r in range(tall):
                    out_ref[owner, w, r * (wide // LANES) + t : r * (wide // LANES) + t + 1, :] = words[
                        w
                    ][left // LANES + t][top + r : top + r + 1, :]


def top_strip_kernel(bricks, *refs):
    planes, _, across = refs[3].shape

    @pl.when(lax.axis_index("strip") == 0)
    def _():
        shade(bricks, jnp.zeros((planes, across), jnp.float32), *refs)


def other_strips_kernel(bricks, *refs):
    *refs, row_above, top_words_ref, out_ref = refs

    @pl.when(lax.axis_index("strip") == 0)
    def _():
        out_ref[...] = top_words_ref[...]

    @pl.when(lax.axis_index("strip") > 0)
    def _():
        shade(bricks, row_above[...].astype(jnp.float32), *refs, out_ref)


def tree_sum(values):
    while len(values) > 1:
        values = [sum(values[i : i + 2]) for i in range(0, len(values), 2)]
    return values[0]


def merge_kernel(planes, before_ref, words_ref, out_ref):
    bricks, _, rows, _ = words_ref.shape
    f32 = jnp.float32
    depth_unit = depth_scale(planes, planes * bricks) / CODE_MAX
    depth, codes = [], []
    for b in range(bricks):
        low, high = words_ref[b, 0], words_ref[b, 1]
        depth.append((low & 0xFFFF).astype(f32) * depth_unit)
        codes.append(
            [lax.shift_right_logical(low, 16), high & 0xFFFF, lax.shift_right_logical(high, 16)]
        )
    terms = [[], [], []]
    for b in range(bricks):
        ahead = tree_sum(
            [before_ref[b, other : other + 1, :] * depth[other] for other in range(bricks) if other != b]
        )
        base = COLOUR_LOW - ahead
        for c in range(3):
            term = jnp.exp2(codes[b][c].astype(f32) * (1.0 / COLOUR_STEPS) + base)
            terms[c].append(jnp.where(codes[b][c] > 0, term, 0.0))
    colour = [tree_sum(values) for values in terms]
    image = colour + [jnp.exp2(-tree_sum(depth))]
    for c in range(4):
        out_ref[pl.ds(c, rows, stride=4), :] = image[c]


def call(kernel, out_shape, *operands, spaces=None, scratch=()):
    vmem = pl.BlockSpec(memory_space=pltpu.VMEM)
    spaces = spaces or {}
    return pl.pallas_call(
        kernel,
        out_shape=out_shape,
        in_specs=[
            pl.BlockSpec(memory_space=spaces.get(i, pltpu.VMEM)) for i in range(len(operands))
        ],
        out_specs=jax.tree.map(lambda _: vmem, out_shape),
        scratch_shapes=scratch,
        compiler_params=pltpu.CompilerParams(vmem_limit_bytes=VMEM_BYTES),
    )(*operands)


def per_device(density, tf_bins, tf_table, brick_order):
    planes, height, across = density.shape
    bricks = lax.axis_size("depth")
    owned = height * across // bricks
    shape = jax.ShapeDtypeStruct
    plane = shape((1, height, across), density.dtype)
    rows = shape((planes, across), density.dtype)
    arguments = [
        pltpu.with_memory_space_constraint(argument, pltpu.HBM)
        for argument in (density, tf_bins, tf_table, brick_order)
    ]
    density, bins, table, order, plane_near, plane_far, row_tail, row_head = call(
        edges_kernel,
        [
            shape(density.shape, density.dtype),
            shape(tf_bins.shape, tf_bins.dtype),
            shape((tf_table.shape[0], LANES), tf_table.dtype),
            shape(brick_order.shape, brick_order.dtype),
            plane,
            plane,
            rows,
            rows,
        ],
        *arguments,
        spaces={i: pltpu.HBM for i in range(4)},
        scratch=[pltpu.VMEM(tf_table.shape, tf_table.dtype), pltpu.SemaphoreType.DMA((4,))],
    )
    plane_far = swap_planes(plane_far, 1)
    plane_near = swap_planes(plane_near, 0)
    row_below = rotate_rows(row_head, -1)
    row_above = rotate_rows(row_tail, 1)
    sheared = shape((planes, 3, height, across), jnp.float32)
    first, second, depth, before = call(
        functools.partial(light_kernel, bricks),
        [
            sheared,
            sheared,
            shape((height, across), jnp.int32),
            shape((bricks, bricks, LANES), jnp.float32),
        ],
        arguments[1],
        bins,
        density,
        table,
        order,
        spaces={0: pltpu.HBM},
        scratch=[pltpu.VMEM(tf_bins.shape, tf_bins.dtype), pltpu.SemaphoreType.DMA],
    )
    words_shape = shape((bricks, 2, owned // LANES, LANES), jnp.int32)
    operands = (plane_far, plane_near, row_below, density, first, second, depth)
    words = call(functools.partial(top_strip_kernel, bricks), words_shape, *operands)
    words = call(
        functools.partial(other_strips_kernel, bricks), words_shape, *operands, row_above, words
    )
    words = lax.all_to_all(words, "depth", 0, 0, tiled=True)
    pieces = owned // LANES
    image = call(
        functools.partial(merge_kernel, planes),
        shape((pieces * 4, LANES), jnp.float32),
        before,
        words,
    )
    return image.reshape(pieces, 4, LANES).transpose(1, 0, 2).reshape(4, owned)


def solution(mesh):
    in_specs = (P("depth", "strip", None), P("depth", "strip", None), P(), P("strip", None))
    out_specs = P(None, ("strip", "depth"))
    return jax.shard_map(
        per_device, mesh=mesh, in_specs=in_specs, out_specs=out_specs, check_vma=False
    )
```
